256 devices in a mesh: dp: 64 (over z, x, core), group: 4 (over y).
Axes of the slice: x: 4, y: 4, z: 8, core: 2. Of those that a mesh axis runs over, the one named last changes fastest.
Arguments:
- embeddings: bfloat16 [262144, 768], P(('dp', 'group')), may hold values from -200 to 200, as said below
- cluster_of: int32 [262144, 1], P(('dp', 'group')), may hold values from 0 to 127; in each aligned block of 1024 rows (0 to 1023, 1024 to 2047, ...) at most 16 rows name the same one
Outputs:
- nearest: float32 [262144], P(('dp', 'group'))
The draws below stay inside these ranges and needn't reach their ends.
Inputs may be any that keep to these rules, and one draw needn't show every extreme that they name: `cluster_of`: among the 1024 rows of one device, at most 16 name one cluster, and in every draw some device has exactly 16 rows of one cluster. `embeddings`: no row is all zeros.
All inputs are finite; a program needn't handle non-finite values.
Results may differ from the reference program's by a relative error of at most 0.00076.
Values may be sent and summed in bfloat16 or wider, within the bound.
A program may use at most 64 MiB of HBM per device.

```python
import math
import jax
import jax.numpy as jnp
import numpy as np
from jax import lax

D = 768
R_DEV = 1024
CLUSTERS = 128
MOST = 16
NROWS = 262144


def draw_embeddings(key, part):
    key = jax.random.fold_in(key, 11)
    key_topic, key_pick, key_strength, key_noise = jax.random.split(key, 4)
    topics = NROWS // 16
    centers = jax.random.normal(key_topic, (topics, D), jnp.float32)
    topic_pick = jax.random.randint(key_pick, (NROWS,), 0, topics)
    strength = jax.random.uniform(key_strength, (NROWS, 1), jnp.float32, 0.5, 2.5)
    noise_part = jax.random.normal(key_noise, (NROWS, D), jnp.float32)
    return (strength * centers[topic_pick] + noise_part).astype(jnp.bfloat16)


def routed_block(own_key, own, number, rows, amount, top, most, lean):
    order = jax.random.permutation(own_key, amount)
    heavy_load, usual = shares(amount, rows * top, most, lean, True), shares(amount, rows * top, most, lean, False)
    places = jnp.arange(amount)

    def named(tallies, rotation):
        used = int((tallies > 0).sum())
        fixed = max(1, used // 4)
        shifted = fixed + (places - fixed + rotation * (used - fixed)) % max(1, amount - fixed)
        return jnp.zeros((amount,), jnp.int32).at[order[jnp.where(places < fixed, places, shifted)]].set(jnp.asarray(tallies, jnp.int32))

    tallies = jnp.where(number % 4 == 0, named(heavy_load, number // 4), named(usual, number - number // 4 - 1))
    mixed = jax.random.permutation(jax.random.fold_in(own, 3), amount)
    giver, taker = mixed[0:amount // 2 * 2:2], mixed[1:amount // 2 * 2:2]
    margin = jnp.minimum(tallies[giver] - 1, most - tallies[taker]) // 2
    margin = jnp.where((giver == order[0]) | (taker == order[0]) | (tallies[taker] == 0), 0, jnp.maximum(margin, 0))
    shifted = jax.random.randint(jax.random.fold_in(own, 4), (amount // 2,), 0, 1 << 20) % (margin + 1)
    tallies = tallies.at[giver].add(-shifted).at[taker].add(shifted)
    items = jnp.searchsorted(jnp.cumsum(tallies), jnp.arange(rows * top), side="right").astype(jnp.int32)
    table = items.reshape(top, rows).T
    table = table[jax.random.permutation(jax.random.fold_in(own, 1), rows)]
    rotation = jax.random.randint(jax.random.fold_in(own, 2), (rows, 1), 0, top)
    return jnp.take_along_axis(table, (jnp.arange(top)[None, :] + rotation) % top, axis=1)


def shares(amount, total, limit, skew, full):
    loads = [(1 << 20) // math.isqrt(grade ** skew) + 1 for grade in range(1, amount + 1)]
    largest = limit if full else min(limit, max(-(-total // amount), total * loads[0] // sum(loads)))
    least = 1 if total - largest >= amount - 1 else 0
    holding, rest = [largest] + [least] * (amount - 1), total - largest - least * (amount - 1)
    while rest > 0:
        free = [i for i in range(1, amount) if holding[i] < largest] or [i for i in range(1, amount) if holding[i] < limit]
        mass, budget = sum([loads[i] for i in free]), rest
        for i in free:
            more = min(limit - holding[i], max(1, budget * loads[i] // mass), rest)
            holding[i] = holding[i] + more
            rest = rest - more
    return np.array(holding)


def setup_inputs(seed: int = 0) -> dict:
    arg_keys = jax.random.split(jax.random.key(seed), 3)
    embeddings = draw_embeddings(jax.random.fold_in(arg_keys[2], 71), 0)
    cluster_of_keys = jax.random.split(jax.random.fold_in(arg_keys[1], 1), NROWS // R_DEV)
    cluster_of_turns = jax.random.permutation(jax.random.fold_in(arg_keys[1], 3), NROWS // R_DEV)
    cluster_of = jax.vmap(lambda own, number: routed_block(jax.random.fold_in(arg_keys[1], 2), own, number, R_DEV, CLUSTERS, 1, MOST, 1))(cluster_of_keys, cluster_of_turns).reshape((NROWS, 1))
    return {"embeddings": embeddings, "cluster_of": cluster_of}


def reference(embeddings, cluster_of):
    widened = embeddings.astype(jnp.float32)
    square_sum = lax.optimization_barrier(jnp.sum(widened * widened, axis=1, keepdims=True))
    unit_rows = (widened / jnp.sqrt(square_sum + 1e-06)).astype(jnp.bfloat16)
    labels = cluster_of[:, 0].astype(jnp.int32)
    count_rows = labels.shape[0]
    sort_order = jnp.argsort(labels, stable=True).astype(jnp.int32)
    sorted_labels = labels[sort_order]
    sorted_unit = unit_rows[sort_order]
    cluster_start = jnp.searchsorted(sorted_labels, sorted_labels, side='left').astype(jnp.int32)
    cluster_end = jnp.searchsorted(sorted_labels, sorted_labels, side='right').astype(jnp.int32)
    tile_size = 512
    tile_count = count_rows // tile_size

    def sorted_block(index):
        low_row = (index * tile_size).astype(jnp.int32)
        own_rows = lax.dynamic_slice_in_dim(sorted_unit, low_row, tile_size, 0)
        own_labels = lax.dynamic_slice_in_dim(sorted_labels, low_row, tile_size, 0)
        row_ids = low_row + jnp.arange(tile_size, dtype=jnp.int32)
        first_tile = cluster_start[low_row] // tile_size
        last_tile = (cluster_end[low_row + tile_size - 1] - 1) // tile_size + 1

        def visit_tile(tile, current):
            low_col = (tile * tile_size).astype(jnp.int32)
            other_rows = lax.dynamic_slice_in_dim(sorted_unit, low_col, tile_size, 0)
            other_labels = lax.dynamic_slice_in_dim(sorted_labels, low_col, tile_size, 0)
            col_ids = low_col + jnp.arange(tile_size, dtype=jnp.int32)
            scores = jnp.dot(own_rows, other_rows.T, preferred_element_type=jnp.float32)
            allowed = (own_labels[:, None] == other_labels[None, :]) & (row_ids[:, None] != col_ids[None, :])
            return jnp.maximum(current, lax.optimization_barrier(jnp.max(jnp.where(allowed, scores, -1.0), axis=1)))
        return lax.fori_loop(first_tile, last_tile, visit_tile, jnp.full((tile_size,), -1.0, jnp.float32))
    sorted_best = lax.map(sorted_block, jnp.arange(tile_count, dtype=jnp.int32)).reshape(-1)
    return jnp.zeros((count_rows,), jnp.float32).at[sort_order].set(sorted_best)
```

```python
import functools

import jax
import jax.numpy as jnp
from jax import lax
from jax.experimental import pallas as pl
from jax.experimental.pallas import tpu as pltpu
from jax.sharding import PartitionSpec as P

MESH = pl.DeviceIdType.MESH
NZ, NX, NY = 8, 4, 4
CHIPS = NZ * NX * NY
CAP = 16
BLK = 256
PER = BLK // CAP
GROUPS = CHIPS // PER
EMPTY = 4.0
LOW = -1e30


def kernel(
    emb_ref, lab_ref, out_ref,
    unit, send, held, twin, acc, res, back, onehot,
    send_sem, recv_sem, fwd_send, fwd_recv, ret_send, ret_recv,
):
    dp = lax.axis_index("dp")
    y = lax.axis_index("group")
    z, x, core = dp // (2 * NX), (dp // 2) % NX, dp % 2
    rows = emb_ref.shape[0]

    def chip_at(r, sign):
        dz, dx, dy = r % NZ, r // (NZ * NY), (r // NZ) % NY
        tz, tx = (z + sign * dz + NZ) % NZ, (x + sign * dx + NX) % NX
        return ((tz * NX + tx) * 2 + core, (y + sign * dy + NY) % NY)

    sibling = ((z * NX + x) * 2 + 1 - core, y)

    barrier = pltpu.get_barrier_semaphore()

    @pl.loop(1, CHIPS)
    def _(r):
        pl.semaphore_signal(barrier, inc=1, device_id=chip_at(r, 1), device_id_type=MESH)

    pl.semaphore_signal(barrier, inc=1, device_id=sibling, device_id_type=MESH)

    @pl.loop(0, rows // BLK)
    def _(i):
        wide = emb_ref[pl.ds(i * BLK, BLK), :].astype(jnp.float32)
        total = jnp.sum(wide * wide, axis=1, keepdims=True)
        unit[pl.ds(i * BLK, BLK), :] = (wide * (1.0 / jnp.sqrt(total + 1e-06))).astype(jnp.bfloat16)

    label = lab_ref[...]
    far_z = (label % NZ - z + NZ) % NZ
    far_x = (label // (NZ * NY) - x + NX) % NX
    far_y = ((label // NZ) % NY - y + NY) % NY
    offset = far_z + NZ * (far_x * NY + far_y)
    hot = offset == lax.broadcasted_iota(jnp.int32, (CHIPS, rows), 0)
    onehot[...] = hot.astype(jnp.bfloat16)
    before = (
        lax.broadcasted_iota(jnp.int32, (rows, rows), 0)
        < lax.broadcasted_iota(jnp.int32, (rows, rows), 1)
    ).astype(jnp.bfloat16)
    earlier = jnp.dot(onehot[...], before, preferred_element_type=jnp.float32)
    rank = jnp.sum(jnp.where(hot, earlier, 0.0), axis=0, keepdims=True).astype(jnp.int32)
    position = offset * CAP + rank

    acc[...] = jnp.full_like(acc, -1.0)

    pl.semaphore_wait(barrier, CHIPS)

    def outgoing(r, g):
        at = pl.ds(pl.multiple_of(r * CAP, CAP), CAP)
        return pltpu.make_async_remote_copy(
            src_ref=send.at[at], dst_ref=held.at[at], send_sem=send_sem, recv_sem=recv_sem.at[g],
            device_id=chip_at(r, 1), device_id_type=MESH,
        )

    @pl.loop(0, GROUPS)
    def _(g):
        base = pl.multiple_of(g * BLK, BLK)
        pick = position == base + lax.broadcasted_iota(jnp.int32, (BLK, rows), 0)
        chosen = pick.astype(jnp.float32)
        filled = jnp.sum(chosen, axis=1, keepdims=True)
        block = jnp.dot(chosen.astype(jnp.bfloat16), unit[...], preferred_element_type=jnp.float32)
        lane = lax.broadcasted_iota(jnp.int32, (BLK, 128), 1)
        mark = jnp.where((lane == 0) & (filled == 0.0), EMPTY, 0.0)
        send[pl.ds(base, BLK), :128] = (block[:, :128] + mark).astype(jnp.bfloat16)
        send[pl.ds(base, BLK), 128:] = block[:, 128:].astype(jnp.bfloat16)

        @pl.loop(1 - jnp.minimum(g, 1), PER)
        def _(k):
            outgoing(g * PER + k, g).start()

    held[:CAP, :] = send[:CAP, :]

    def forward(g):
        at = pl.ds(pl.multiple_of(g * BLK, BLK), BLK)
        return pltpu.make_async_remote_copy(
            src_ref=held.at[at], dst_ref=twin.at[at], send_sem=fwd_send, recv_sem=fwd_recv.at[g],
            device_id=sibling, device_id_type=MESH,
        )

    def meet(others, j, i, same):
        at = pl.ds(pl.multiple_of(i * BLK, BLK), BLK)
        other = others[pl.ds(pl.multiple_of(j * BLK, BLK), BLK), :]
        score = lax.dot_general(
            other, held[at, :], (((1,), (1,)), ((), ())), preferred_element_type=jnp.float32
        )
        score = score + jnp.where(other[:, 0:1].astype(jnp.float32) > 2.0, LOW, 0.0)
        if same:
            one = lax.broadcasted_iota(jnp.int32, (BLK, BLK), 0)
            two = lax.broadcasted_iota(jnp.int32, (BLK, BLK), 1)
            score = jnp.where(one == two, LOW, score)
        best = jnp.max(score.reshape(BLK // 8, 8, BLK), axis=0)
        acc[:, at] = jnp.maximum(acc[:, at], best)

    def arrive(g, first):
        taken = PER - 1 if first else PER
        start = CAP if first else g * BLK
        at = pl.ds(start if first else pl.multiple_of(start, BLK), taken * CAP)
        pltpu.make_async_copy(held.at[at], held.at[at], recv_sem.at[g]).wait()

    arrive(0, True)
    forward(0).start()
    meet(held, 0, 0, True)

    @pl.loop(1, GROUPS)
    def _(g):
        arrive(g, False)
        forward(g).start()
        meet(held, g, g, True)

        @pl.loop(0, g)
        def _(i):
            meet(held, g, i, False)
            meet(held, i, g, False)

        @pl.loop(0, g - 1)
        def _(j):
            meet(twin, j, g, False)

        forward(g - 1).wait_recv()

        @pl.loop(0, g + 1)
        def _(i):
            meet(twin, g - 1, i, False)

    forward(GROUPS - 1).wait_recv()

    def returning(r):
        return pltpu.make_async_remote_copy(
            src_ref=res.at[r // 8], dst_ref=back.at[r], send_sem=ret_send, recv_sem=ret_recv,
            device_id=chip_at(r, -1), device_id_type=MESH,
        )

    for i in range(GROUPS):
        meet(twin, GROUPS - 1, i, False)
        best = jnp.max(acc[:, i * BLK:(i + 1) * BLK], axis=0, keepdims=True)
        res[2 * i] = best[:, :128]
        res[2 * i + 1] = best[:, 128:]

        @pl.loop(1 if i == 0 else 0, PER)
        def _(k):
            returning(i * PER + k).start()

    back[0] = res[0]
    pltpu.make_async_copy(back.at[pl.ds(1, CHIPS - 1)], back.at[pl.ds(1, CHIPS - 1)], ret_recv).wait()

    got = back[...].reshape(CHIPS, 128)
    high = got.astype(jnp.bfloat16)
    rest = got - high.astype(jnp.float32)
    mid = rest.astype(jnp.bfloat16)
    low = (rest - mid.astype(jnp.float32)).astype(jnp.bfloat16)
    spread = jnp.zeros((128, rows), jnp.float32)
    for part in (high, mid, low):
        spread += lax.dot_general(
            part, onehot[...], (((0,), (0,)), ((), ())), preferred_element_type=jnp.float32
        )
    place = (offset % 8) * CAP + rank
    chosen = place == lax.broadcasted_iota(jnp.int32, (128, rows), 0)
    out_ref[...] = jnp.sum(jnp.where(chosen, spread, 0.0), axis=0, keepdims=True)

    pltpu.make_async_copy(send.at[pl.ds(CAP, (CHIPS - 1) * CAP)], send.at[pl.ds(CAP, (CHIPS - 1) * CAP)], send_sem).wait()
    pltpu.make_async_copy(held, held, fwd_send).wait()
    pltpu.make_async_copy(back.at[pl.ds(1, CHIPS - 1)], back.at[pl.ds(1, CHIPS - 1)], ret_send).wait()


def on_device(embeddings, cluster_of):
    rows, features = embeddings.shape
    slots = CHIPS * CAP
    nearest = pl.pallas_call(
        kernel,
        out_shape=jax.ShapeDtypeStruct((1, rows), jnp.float32),
        in_specs=[pl.BlockSpec(memory_space=pltpu.VMEM)] * 2,
        out_specs=pl.BlockSpec(memory_space=pltpu.VMEM),
        scratch_shapes=[
            pltpu.VMEM((rows, features), jnp.bfloat16),
            pltpu.VMEM((slots, features), jnp.bfloat16),
            pltpu.VMEM((slots, features), jnp.bfloat16),
            pltpu.VMEM((slots, features), jnp.bfloat16),
            pltpu.VMEM((8, slots), jnp.float32),
            pltpu.VMEM((CHIPS // 8, 1, 128), jnp.float32),
            pltpu.VMEM((CHIPS, 1, 128), jnp.float32),
            pltpu.VMEM((CHIPS, rows), jnp.bfloat16),
            pltpu.SemaphoreType.DMA,
            pltpu.SemaphoreType.DMA((GROUPS,)),
            pltpu.SemaphoreType.DMA,
            pltpu.SemaphoreType.DMA((GROUPS,)),
            pltpu.SemaphoreType.DMA,
            pltpu.SemaphoreType.DMA,
        ],
        compiler_params=pltpu.CompilerParams(
            collective_id=0, has_side_effects=True, vmem_limit_bytes=48 << 20
        ),
        cost_estimate=pl.CostEstimate(
            flops=2 * slots * 2 * slots * features, bytes_accessed=2 * rows * features, transcendentals=0
        ),
    )(embeddings, cluster_of.reshape(1, rows))
    return nearest.reshape(rows)


def solution(mesh):
    return jax.shard_map(
        on_device,
        mesh=mesh,
        in_specs=(P(("dp", "group"), None), P(("dp", "group"), None)),
        out_specs=P(("dp", "group")),
        check_vma=False,
    )
```

```python
import jax
import jax.numpy as jnp
from jax import lax
from jax.experimental import pallas as pl
from jax.experimental.pallas import tpu as pltpu
from jax.sharding import PartitionSpec as P

MESH = pl.DeviceIdType.MESH
NZ, NX, NY = 8, 4, 4
PLANE = NX * NY
CHIPS = NZ * PLANE
CAP = 16
GRP = NZ * CAP
PAIR = 2 * GRP
BOTH = 2 * PAIR
PAIRS = PLANE // 2
EARLY = 4
EMPTY = 4.0
LOW = -1e30
LANES = 128


def kernel(
    emb_hbm, lab_hbm, out_ref,
    emb, lab, send, pool, acc, res, mid, back, onehot,
    emb_sem, lab_sem, send_sem, recv_sem, fwd_send, fwd_recv, one_send, one_recv, two_send, two_recv,
):
    dp = lax.axis_index("dp")
    y = lax.axis_index("group")
    z, x, core = dp // (2 * NX), (dp // 2) % NX, dp % 2
    rows = emb.shape[0]
    quarter = rows // 4

    def loading(i):
        at = pl.ds(i * quarter, quarter)
        return pltpu.make_async_copy(emb_hbm.at[at], emb.at[at], emb_sem.at[i])

    labels = pltpu.make_async_copy(lab_hbm, lab, lab_sem)
    labels.start()
    for i in range(4):
        loading(i).start()

    z_ahead = [((z + d) % NZ) * (2 * NX) + core for d in range(NZ)]
    z_behind = [((z + NZ - d) % NZ) * (2 * NX) + core for d in range(NZ)]

    def ahead(d, p):
        return (z_ahead[d] + ((x + p // NY) % NX) * 2, (y + p % NY) % NY)

    def plane_behind(p):
        return (z_behind[0] + ((x + NX - p // NY) % NX) * 2, (y + NY - p % NY) % NY)

    def column_behind(d):
        return (z_behind[d] + x * 2, y)

    sibling = ((z * NX + x) * 2 + 1 - core, y)

    barrier = pltpu.get_barrier_semaphore()

    def greet(d, p):
        pl.semaphore_signal(barrier, inc=1, device_id=ahead(d, p), device_id_type=MESH)

    for d in range(1, NZ):
        greet(d, 0)

    @pl.loop(1, PLANE)
    def _(p):
        for d in range(NZ):
            greet(d, p)

    pl.semaphore_signal(barrier, inc=1, device_id=sibling, device_id_type=MESH)

    labels.wait()
    label = lab[...]
    far_z = (label % NZ - z + NZ) % NZ
    far_x = (label // PLANE // 2 - x + NX) % NX
    far_y = ((label // NZ) % NY - y + NY) % NY
    plane = far_x * NY + far_y
    hot = far_z * PLANE + plane == lax.broadcasted_iota(jnp.int32, (CHIPS, rows), 0)
    ones = hot.astype(jnp.bfloat16)
    onehot[...] = ones
    row = lax.broadcasted_iota(jnp.int32, (LANES, 2 * LANES), 0)
    col = lax.broadcasted_iota(jnp.int32, (LANES, 2 * LANES), 1)
    before = ((row < col) | (col >= LANES)).astype(jnp.bfloat16)
    ranks = []
    carry = jnp.zeros((CHIPS, LANES), jnp.float32)
    for t in range(rows // LANES):
        at = slice(t * LANES, (t + 1) * LANES)
        both = jnp.dot(ones[:, at], before, preferred_element_type=jnp.float32)
        earlier = jnp.where(hot[:, at], both[:, :LANES] + carry, 0.0)
        carry = carry + both[:, LANES:]
        ranks.append(jnp.sum(earlier, axis=0, keepdims=True))
    rank = jnp.concatenate(ranks, axis=1).astype(jnp.int32)
    position = (plane * NZ + far_z) * CAP + rank

    acc[...] = jnp.full_like(acc, -1.0)

    for i in range(4):
        loading(i).wait()

    def dispatch(h):
        base = pl.multiple_of(h * PAIR, PAIR)
        pick = position == base + lax.broadcasted_iota(jnp.int32, (PAIR, rows), 0)
        chosen = jnp.where(pick, 1.0, 0.0)
        filled = jnp.sum(chosen, axis=1, keepdims=True)
        wide = jnp.dot(chosen.astype(jnp.bfloat16), emb[...], preferred_element_type=jnp.float32)
        total = jnp.sum(wide * wide, axis=1, keepdims=True)
        wide = wide * (1.0 / jnp.sqrt(total + 1e-06))
        lane = lax.broadcasted_iota(jnp.int32, (PAIR, LANES), 1)
        mark = jnp.where((lane == 0) & (filled == 0.0), EMPTY, 0.0)
        send[pl.ds(base, PAIR), :LANES] = (wide[:, :LANES] + mark).astype(jnp.bfloat16)
        send[pl.ds(base, PAIR), LANES:] = wide[:, LANES:].astype(jnp.bfloat16)

    def outgoing(d, p):
        src = pl.ds(pl.multiple_of(p * GRP + d * CAP, CAP), CAP)
        dst = pl.ds(pl.multiple_of((p // 2) * BOTH + (p % 2) * GRP + d * CAP, CAP), CAP)
        return pltpu.make_async_remote_copy(
            src_ref=send.at[src], dst_ref=pool.at[dst], send_sem=send_sem, recv_sem=recv_sem.at[p],
            device_id=ahead(d, p), device_id_type=MESH,
        )

    @pl.loop(0, EARLY)
    def _(h):
        dispatch(h)

    pl.semaphore_wait(barrier, CHIPS)

    pltpu.make_async_copy(send.at[pl.ds(0, CAP)], pool.at[pl.ds(0, CAP)], recv_sem.at[0]).start()
    for d in range(1, NZ):
        outgoing(d, 0).start()

    @pl.loop(1, 2 * EARLY)
    def _(p):
        for d in range(NZ):
            outgoing(d, p).start()

    @pl.loop(EARLY, PAIRS)
    def _(h):
        dispatch(h)
        for odd in range(2):
            for d in range(NZ):
                outgoing(d, 2 * h + odd).start()

    def mine(h, odd):
        return pl.ds(pl.multiple_of(h * BOTH + odd * GRP, GRP), GRP)

    def theirs(h, odd):
        return pl.ds(pl.multiple_of(h * BOTH + PAIR + odd * GRP, GRP), GRP)

    def forward(h, odd):
        g = 2 * h + odd
        return pltpu.make_async_remote_copy(
            src_ref=pool.at[mine(h, odd)], dst_ref=pool.at[theirs(h, odd)],
            send_sem=fwd_send, recv_sem=fwd_recv.at[g], device_id=sibling, device_id_type=MESH,
        )

    def arrive(h, odd):
        at = mine(h, odd)
        pltpu.make_async_copy(pool.at[at], pool.at[at], recv_sem.at[2 * h + odd]).wait()

    def meet(other, i, same):
        own = pool[pl.ds(pl.multiple_of(i * BOTH, BOTH), PAIR), :]
        score = lax.dot_general(other, own, (((1,), (1,)), ((), ())), preferred_element_type=jnp.float32)
        score = score + jnp.where(other[:, 0:1].astype(jnp.float32) > 2.0, LOW, 0.0)
        if same:
            one = lax.broadcasted_iota(jnp.int32, score.shape, 0)
            two = lax.broadcasted_iota(jnp.int32, score.shape, 1)
            score = jnp.where(one == two, LOW, score)
        best = jnp.max(score.reshape(score.shape[0] // 8, 8, PAIR), axis=0)
        at = pl.ds(pl.multiple_of(i * PAIR, PAIR), PAIR)
        acc[:, at] = jnp.maximum(acc[:, at], best)

    def whole(h):
        return pool[pl.ds(pl.multiple_of(h * BOTH, BOTH), BOTH), :]

    def newest(h, odd):
        return jnp.concatenate([pool[mine(h, odd), :], pool[theirs(h, odd), :]], axis=0)

    def even_step(h):
        arrive(h, 0)
        forward(h, 0).start()
        forward(h, 0).wait_recv()

        @pl.loop(0, h)
        def _(i):
            meet(newest(h, 0), i, False)

        arrive(h, 1)
        forward(h, 1).start()

        @pl.loop(0, h)
        def _(j):
            meet(whole(j), h, False)

        forward(h, 1).wait_recv()

    @pl.loop(0, PAIRS - 1)
    def _(h):
        even_step(h)

        @pl.loop(0, h)
        def _(i):
            meet(newest(h, 1), i, False)

        meet(whole(h), h, True)

    last = PAIRS - 1
    even_step(last)

    def in_plane(p):
        return pltpu.make_async_remote_copy(
            src_ref=res.at[p], dst_ref=mid.at[p], send_sem=one_send, recv_sem=one_recv,
            device_id=plane_behind(p), device_id_type=MESH,
        )

    def finish(i, first):
        best = jnp.max(acc[:, pl.ds(pl.multiple_of(i * PAIR, PAIR), PAIR)], axis=0, keepdims=True)
        for odd in range(2):
            res[2 * i + odd] = best[:, odd * LANES:(odd + 1) * LANES]
            if first and odd == 0:
                mid[0] = best[:, :LANES]
            else:
                in_plane(2 * i + odd).start()

    meet(newest(last, 1), 0, False)
    finish(0, True)

    @pl.loop(1, last)
    def _(i):
        meet(newest(last, 1), i, False)
        finish(i, False)

    meet(whole(last), last, True)
    finish(last, False)

    rest = pl.ds(1, PLANE - 1)
    pltpu.make_async_copy(mid.at[rest], mid.at[rest], one_recv).wait()
    for d in range(1, NZ):
        pltpu.make_async_remote_copy(
            src_ref=mid, dst_ref=back.at[pl.ds(d * PLANE, PLANE)], send_sem=two_send, recv_sem=two_recv,
            device_id=column_behind(d), device_id_type=MESH,
        ).start()
    back[:PLANE] = mid[...]
    far = pl.ds(PLANE, CHIPS - PLANE)
    pltpu.make_async_copy(back.at[far], back.at[far], two_recv).wait()

    got = back[...].reshape(CHIPS, LANES)
    high = got.astype(jnp.bfloat16)
    rest_of = got - high.astype(jnp.float32)
    middle = rest_of.astype(jnp.bfloat16)
    low = (rest_of - middle.astype(jnp.float32)).astype(jnp.bfloat16)
    spread = jnp.zeros((LANES, rows), jnp.float32)
    for part in (high, middle, low):
        spread += lax.dot_general(
            part, onehot[...], (((0,), (0,)), ((), ())), preferred_element_type=jnp.float32
        )
    place = far_z * CAP + rank
    chosen = place == lax.broadcasted_iota(jnp.int32, (LANES, rows), 0)
    out_ref[...] = jnp.sum(jnp.where(chosen, spread, 0.0), axis=0, keepdims=True)

    sent = pl.ds(CAP, (CHIPS - 1) * CAP)
    pltpu.make_async_copy(send.at[sent], send.at[sent], send_sem).wait()
    half = pl.ds(0, PLANE * GRP)
    pltpu.make_async_copy(pool.at[half], pool.at[half], fwd_send).wait()
    pltpu.make_async_copy(res.at[rest], res.at[rest], one_send).wait()
    pltpu.make_async_copy(back.at[far], back.at[far], two_send).wait()


def on_device(embeddings, cluster_of):
    rows, features = embeddings.shape
    slots = CHIPS * CAP
    nearest = pl.pallas_call(
        kernel,
        out_shape=jax.ShapeDtypeStruct((1, rows), jnp.float32),
        in_specs=[pl.BlockSpec(memory_space=pltpu.HBM)] * 2,
        out_specs=pl.BlockSpec(memory_space=pltpu.VMEM),
        scratch_shapes=[
            pltpu.VMEM((rows, features), jnp.bfloat16),
            pltpu.VMEM((1, rows), jnp.int32),
            pltpu.VMEM((slots, features), jnp.bfloat16),
            pltpu.VMEM((2 * slots, features), jnp.bfloat16),
            pltpu.VMEM((8, slots), jnp.float32),
            pltpu.VMEM((PLANE, 1, LANES), jnp.float32),
            pltpu.VMEM((PLANE, 1, LANES), jnp.float32),
            pltpu.VMEM((CHIPS, 1, LANES), jnp.float32),
            pltpu.VMEM((CHIPS, rows), jnp.bfloat16),
            pltpu.SemaphoreType.DMA((4,)),
            pltpu.SemaphoreType.DMA,
            pltpu.SemaphoreType.DMA,
            pltpu.SemaphoreType.DMA((PLANE,)),
            pltpu.SemaphoreType.DMA,
            pltpu.SemaphoreType.DMA((PLANE,)),
            pltpu.SemaphoreType.DMA,
            pltpu.SemaphoreType.DMA,
            pltpu.SemaphoreType.DMA,
            pltpu.SemaphoreType.DMA,
        ],
        compiler_params=pltpu.CompilerParams(
            collective_id=0, has_side_effects=True, vmem_limit_bytes=56 << 20
        ),
        cost_estimate=pl.CostEstimate(
            flops=2 * slots * 2 * slots * features, bytes_accessed=2 * rows * features, transcendentals=0
        ),
    )(embeddings, cluster_of.reshape(1, rows))
    return nearest.reshape(rows)


def solution(mesh):
    return jax.shard_map(
        on_device,
        mesh=mesh,
        in_specs=(P(("dp", "group"), None), P(("dp", "group"), None)),
        out_specs=P(("dp", "group")),
        check_vma=False,
    )
```

```python
import jax
import jax.numpy as jnp
from jax import lax
from jax.experimental import pallas as pl
from jax.experimental.pallas import tpu as pltpu
from jax.sharding import PartitionSpec as P

MESH = pl.DeviceIdType.MESH
NZ, NX, NY = 8, 4, 4
PLANE = NX * NY
CHIPS = NZ * PLANE
CAP = 16
GRP = NZ * CAP
PAIR = 2 * GRP
BOTH = 2 * PAIR
PAIRS = PLANE // 2
EARLY = 2
EMPTY = 4.0
LOW = -1e30
LANES = 128


def kernel(
    emb_hbm, lab_hbm, out_ref,
    emb, lab, send, pool, acc, res, back, onehot,
    emb_sem, lab_sem, send_sem, recv_sem, fwd_send, fwd_recv, ret_send, ret_recv,
):
    dp = lax.axis_index("dp")
    y = lax.axis_index("group")
    z, x, core = dp // (2 * NX), (dp // 2) % NX, dp % 2
    rows = emb.shape[0]
    quarter = rows // 4

    def loading(i):
        at = pl.ds(i * quarter, quarter)
        return pltpu.make_async_copy(emb_hbm.at[at], emb.at[at], emb_sem.at[i])

    labels = pltpu.make_async_copy(lab_hbm, lab, lab_sem)
    labels.start()
    for i in range(4):
        loading(i).start()

    z_ahead = [((z + d) % NZ) * (2 * NX) + core for d in range(NZ)]
    z_behind = [((z + NZ - d) % NZ) * (2 * NX) + core for d in range(NZ)]

    def ahead(d, g):
        p = PLANE - 1 - g
        return (z_ahead[d] + ((x + p // NY) % NX) * 2, (y + p % NY) % NY)

    def behind(d, g):
        p = PLANE - 1 - g
        return (z_behind[d] + ((x + NX - p // NY) % NX) * 2, (y + NY - p % NY) % NY)

    sibling = ((z * NX + x) * 2 + 1 - core, y)

    barrier = pltpu.get_barrier_semaphore()

    def greet(d, g):
        pl.semaphore_signal(barrier, inc=1, device_id=ahead(d, g), device_id_type=MESH)

    @pl.loop(0, PLANE - 1)
    def _(g):
        for d in range(NZ):
            greet(d, g)

    for d in range(1, NZ):
        greet(d, PLANE - 1)

    pl.semaphore_signal(barrier, inc=1, device_id=sibling, device_id_type=MESH)

    labels.wait()
    label = lab[...]
    far_z = (label % NZ - z + NZ) % NZ
    far_x = (label // PLANE // 2 - x + NX) % NX
    far_y = ((label // NZ) % NY - y + NY) % NY
    chip = (PLANE - 1 - far_x * NY - far_y) * NZ + far_z
    hot = chip == lax.broadcasted_iota(jnp.int32, (CHIPS, rows), 0)
    ones = hot.astype(jnp.bfloat16)
    onehot[...] = ones
    row = lax.broadcasted_iota(jnp.int32, (LANES, 2 * LANES), 0)
    col = lax.broadcasted_iota(jnp.int32, (LANES, 2 * LANES), 1)
    before = ((row < col) | (col >= LANES)).astype(jnp.bfloat16)
    ranks = []
    carry = jnp.zeros((CHIPS, LANES), jnp.float32)
    for t in range(rows // LANES):
        at = slice(t * LANES, (t + 1) * LANES)
        both = jnp.dot(ones[:, at], before, preferred_element_type=jnp.float32)
        earlier = jnp.where(hot[:, at], both[:, :LANES] + carry, 0.0)
        carry = carry + both[:, LANES:]
        ranks.append(jnp.sum(earlier, axis=0, keepdims=True))
    rank = jnp.concatenate(ranks, axis=1).astype(jnp.int32)
    position = chip * CAP + rank

    acc[...] = jnp.full_like(acc, -1.0)

    for i in range(4):
        loading(i).wait()

    def dispatch(h):
        base = pl.multiple_of(h * PAIR, PAIR)
        pick = position == base + lax.broadcasted_iota(jnp.int32, (PAIR, rows), 0)
        chosen = jnp.where(pick, 1.0, 0.0)
        filled = jnp.sum(chosen, axis=1, keepdims=True)
        wide = jnp.dot(chosen.astype(jnp.bfloat16), emb[...], preferred_element_type=jnp.float32)
        total = jnp.sum(wide * wide, axis=1, keepdims=True)
        wide = wide * (1.0 / jnp.sqrt(total + 1e-06))
        lane = lax.broadcasted_iota(jnp.int32, (PAIR, LANES), 1)
        mark = jnp.where((lane == 0) & (filled == 0.0), EMPTY, 0.0)
        send[pl.ds(base, PAIR), :LANES] = (wide[:, :LANES] + mark).astype(jnp.bfloat16)
        send[pl.ds(base, PAIR), LANES:] = wide[:, LANES:].astype(jnp.bfloat16)

    def outgoing(d, h, odd):
        g = 2 * h + odd
        src = pl.ds(pl.multiple_of(g * GRP + d * CAP, CAP), CAP)
        dst = pl.ds(pl.multiple_of(h * BOTH + odd * GRP + d * CAP, CAP), CAP)
        return pltpu.make_async_remote_copy(
            src_ref=send.at[src], dst_ref=pool.at[dst], send_sem=send_sem, recv_sem=recv_sem.at[g],
            device_id=ahead(d, g), device_id_type=MESH,
        )

    def send_pair(h):
        for odd in range(2):
            for d in range(NZ):
                outgoing(d, h, odd).start()

    @pl.loop(0, EARLY)
    def _(h):
        dispatch(h)

    pl.semaphore_wait(barrier, CHIPS)

    @pl.loop(0, EARLY)
    def _(h):
        send_pair(h)

    @pl.loop(EARLY, PAIRS - 1)
    def _(h):
        dispatch(h)
        send_pair(h)

    dispatch(PAIRS - 1)
    for d in range(NZ):
        outgoing(d, PAIRS - 1, 0).start()
    own_src = pl.ds((PLANE - 1) * GRP, CAP)
    own_dst = pl.ds((PAIRS - 1) * BOTH + GRP, CAP)
    pltpu.make_async_copy(send.at[own_src], pool.at[own_dst], recv_sem.at[PLANE - 1]).start()
    for d in range(1, NZ):
        outgoing(d, PAIRS - 1, 1).start()

    def mine(h, odd):
        return pl.ds(pl.multiple_of(h * BOTH + odd * GRP, GRP), GRP)

    def theirs(h, odd):
        return pl.ds(pl.multiple_of(h * BOTH + PAIR + odd * GRP, GRP), GRP)

    def forward(h, odd):
        g = 2 * h + odd
        return pltpu.make_async_remote_copy(
            src_ref=pool.at[mine(h, odd)], dst_ref=pool.at[theirs(h, odd)],
            send_sem=fwd_send, recv_sem=fwd_recv.at[g], device_id=sibling, device_id_type=MESH,
        )

    def arrive(h, odd):
        at = mine(h, odd)
        pltpu.make_async_copy(pool.at[at], pool.at[at], recv_sem.at[2 * h + odd]).wait()

    def meet(other, i, same):
        own = pool[pl.ds(pl.multiple_of(i * BOTH, BOTH), PAIR), :]
        score = lax.dot_general(other, own, (((1,), (1,)), ((), ())), preferred_element_type=jnp.float32)
        score = score + jnp.where(other[:, 0:1].astype(jnp.float32) > 2.0, LOW, 0.0)
        if same:
            one = lax.broadcasted_iota(jnp.int32, score.shape, 0)
            two = lax.broadcasted_iota(jnp.int32, score.shape, 1)
            score = jnp.where(one == two, LOW, score)
        best = jnp.max(score.reshape(score.shape[0] // 8, 8, PAIR), axis=0)
        at = pl.ds(pl.multiple_of(i * PAIR, PAIR), PAIR)
        acc[:, at] = jnp.maximum(acc[:, at], best)

    def whole(h):
        return pool[pl.ds(pl.multiple_of(h * BOTH, BOTH), BOTH), :]

    def newest(h, odd):
        return jnp.concatenate([pool[mine(h, odd), :], pool[theirs(h, odd), :]], axis=0)

    def even_step(h):
        arrive(h, 0)
        forward(h, 0).start()
        forward(h, 0).wait_recv()

        @pl.loop(0, h)
        def _(i):
            meet(newest(h, 0), i, False)

        arrive(h, 1)
        forward(h, 1).start()

        @pl.loop(0, h)
        def _(j):
            meet(whole(j), h, False)

        forward(h, 1).wait_recv()

    @pl.loop(0, PAIRS - 1)
    def _(h):
        even_step(h)

        @pl.loop(0, h)
        def _(i):
            meet(newest(h, 1), i, False)

        meet(whole(h), h, True)

    last = PAIRS - 1

    def returning(d, g):
        return pltpu.make_async_remote_copy(
            src_ref=res.at[g], dst_ref=back.at[g * NZ + d], send_sem=ret_send, recv_sem=ret_recv,
            device_id=behind(d, g), device_id_type=MESH,
        )

    def finish(i):
        best = jnp.max(acc[:, i * PAIR:(i + 1) * PAIR], axis=0, keepdims=True)
        for odd in range(2):
            g = 2 * i + odd
            res[g] = best[:, odd * LANES:(odd + 1) * LANES]
            for d in range(NZ):
                if g == PLANE - 1 and d == 0:
                    pltpu.make_async_copy(res.at[g], back.at[g * NZ], ret_recv).start()
                else:
                    returning(d, g).start()

    arrive(last, 0)
    forward(last, 0).start()
    forward(last, 0).wait_recv()

    @pl.loop(0, last)
    def _(i):
        meet(newest(last, 0), i, False)

    arrive(last, 1)
    forward(last, 1).start()
    for j in range(last):
        meet(whole(j), last, False)
    forward(last, 1).wait_recv()
    for i in range(last):
        meet(newest(last, 1), i, False)
        finish(i)
    meet(whole(last), last, True)
    finish(last)

    pltpu.make_async_copy(back, back, ret_recv).wait()

    got = back[...].reshape(CHIPS, LANES)
    high = got.astype(jnp.bfloat16)
    rest = got - high.astype(jnp.float32)
    middle = rest.astype(jnp.bfloat16)
    low = (rest - middle.astype(jnp.float32)).astype(jnp.bfloat16)
    spread = jnp.zeros((LANES, rows), jnp.float32)
    for part in (high, middle, low):
        spread += lax.dot_general(
            part, onehot[...], (((0,), (0,)), ((), ())), preferred_element_type=jnp.float32
        )
    place = far_z * CAP + rank
    chosen = place == lax.broadcasted_iota(jnp.int32, (LANES, rows), 0)
    out_ref[...] = jnp.sum(jnp.where(chosen, spread, 0.0), axis=0, keepdims=True)

    sent = pl.ds(CAP, (CHIPS - 1) * CAP)
    pltpu.make_async_copy(send.at[sent], send.at[sent], send_sem).wait()
    half = pl.ds(0, PLANE * GRP)
    pltpu.make_async_copy(pool.at[half], pool.at[half], fwd_send).wait()
    others = pl.ds(0, CHIPS - 1)
    pltpu.make_async_copy(back.at[others], back.at[others], ret_send).wait()


def on_device(embeddings, cluster_of):
    rows, features = embeddings.shape
    slots = CHIPS * CAP
    nearest = pl.pallas_call(
        kernel,
        out_shape=jax.ShapeDtypeStruct((1, rows), jnp.float32),
        in_specs=[pl.BlockSpec(memory_space=pltpu.HBM)] * 2,
        out_specs=pl.BlockSpec(memory_space=pltpu.VMEM),
        scratch_shapes=[
            pltpu.VMEM((rows, features), jnp.bfloat16),
            pltpu.VMEM((1, rows), jnp.int32),
            pltpu.VMEM((slots, features), jnp.bfloat16),
            pltpu.VMEM((2 * slots, features), jnp.bfloat16),
            pltpu.VMEM((8, slots), jnp.float32),
            pltpu.VMEM((PLANE, 1, LANES), jnp.float32),
            pltpu.VMEM((CHIPS, 1, LANES), jnp.float32),
            pltpu.VMEM((CHIPS, rows), jnp.bfloat16),
            pltpu.SemaphoreType.DMA((4,)),
            pltpu.SemaphoreType.DMA,
            pltpu.SemaphoreType.DMA,
            pltpu.SemaphoreType.DMA((PLANE,)),
            pltpu.SemaphoreType.DMA,
            pltpu.SemaphoreType.DMA((PLANE,)),
            pltpu.SemaphoreType.DMA,
            pltpu.SemaphoreType.DMA,
        ],
        compiler_params=pltpu.CompilerParams(
            collective_id=0, has_side_effects=True, vmem_limit_bytes=56 << 20
        ),
        cost_estimate=pl.CostEstimate(
            flops=2 * slots * 2 * slots * features, bytes_accessed=2 * rows * features, transcendentals=0
        ),
    )(embeddings, cluster_of.reshape(1, rows))
    return nearest.reshape(rows)


def solution(mesh):
    return jax.shard_map(
        on_device,
        mesh=mesh,
        in_specs=(P(("dp", "group"), None), P(("dp", "group"), None)),
        out_specs=P(("dp", "group")),
        check_vma=False,
    )
```

```python
import jax
import jax.numpy as jnp
from jax import lax
from jax.experimental import pallas as pl
from jax.experimental.pallas import tpu as pltpu
from jax.sharding import PartitionSpec as P

MESH = pl.DeviceIdType.MESH
NZ, NX, NY = 8, 4, 4
PLANE = NX * NY
CHIPS = NZ * PLANE
CAP = 16
GRP = NZ * CAP
PAIR = 2 * GRP
BOTH = 2 * PAIR
PAIRS = PLANE // 2
EARLY = 2
REACH = 3
EMPTY = 4.0
LOW = -1e30
LANES = 128


def hops(d, g):
    p = PLANE - 1 - g
    return sum(min(a, n - a) for a, n in ((d, NZ), (p // NY, NX), (p % NY, NY)))


OFFSETS = [(d, g) for g in range(PLANE) for d in range(NZ) if hops(d, g)]
NEAR = [o for o in OFFSETS if hops(*o) <= REACH]
FAR = [o for o in OFFSETS if hops(*o) > REACH]


def kernel(
    emb_hbm, lab_ref, out_ref,
    emb, send, pool, acc, res, back, onehot,
    emb_sem, near_sem, far_sem, send_sem, recv_sem, fwd_send, fwd_recv, ret_send, ret_recv,
):
    dp = lax.axis_index("dp")
    y = lax.axis_index("group")
    z, x, core = dp // (2 * NX), (dp // 2) % NX, dp % 2
    rows = emb.shape[0]
    quarter = rows // 4

    def loading(i):
        at = pl.ds(i * quarter, quarter)
        return pltpu.make_async_copy(emb_hbm.at[at], emb.at[at], emb_sem.at[i])

    for i in range(4):
        loading(i).start()

    z_ahead = [((z + d) % NZ) * (2 * NX) + core for d in range(NZ)]
    z_behind = [((z + NZ - d) % NZ) * (2 * NX) + core for d in range(NZ)]

    x_ahead = [((x + d) % NX) * 2 for d in range(NX)]
    y_ahead = [(y + d) % NY for d in range(NY)]

    def ahead(d, g):
        p = PLANE - 1 - g
        return (z_ahead[d] + x_ahead[p // NY], y_ahead[p % NY])

    def behind(d, g):
        p = PLANE - 1 - g
        return (z_behind[d] + x_ahead[-(p // NY)], y_ahead[-(p % NY)])

    sibling = ((z * NX + x) * 2 + 1 - core, y)

    barrier = pltpu.get_barrier_semaphore()

    def greet(d, g, counter):
        chip, along = ahead(d, g)
        pl.semaphore_signal(
            barrier, inc=1, device_id=(chip - core + counter, along), device_id_type=MESH
        )

    pl.semaphore_signal(barrier, inc=1, device_id=sibling, device_id_type=MESH)
    for offset in FAR:
        greet(*offset, 1)
    for offset in NEAR:
        greet(*offset, 0)

    label = lab_ref[...]
    far_z = (label % NZ - z + NZ) % NZ
    far_x = (label // PLANE // 2 - x + NX) % NX
    far_y = ((label // NZ) % NY - y + NY) % NY
    chip = (PLANE - 1 - far_x * NY - far_y) * NZ + far_z
    hot = chip == lax.broadcasted_iota(jnp.int32, (CHIPS, rows), 0)
    ones = hot.astype(jnp.bfloat16)
    onehot[...] = ones
    row = lax.broadcasted_iota(jnp.int32, (LANES, 2 * LANES), 0)
    col = lax.broadcasted_iota(jnp.int32, (LANES, 2 * LANES), 1)
    before = ((row < col) | (col >= LANES)).astype(jnp.bfloat16)
    ranks = []
    carry = jnp.zeros((CHIPS, LANES), jnp.float32)
    for t in range(rows // LANES):
        at = slice(t * LANES, (t + 1) * LANES)
        both = jnp.dot(ones[:, at], before, preferred_element_type=jnp.float32)
        earlier = jnp.where(hot[:, at], both[:, :LANES] + carry, 0.0)
        carry = carry + both[:, LANES:]
        ranks.append(jnp.sum(earlier, axis=0, keepdims=True))
    rank = jnp.concatenate(ranks, axis=1).astype(jnp.int32)
    position = chip * CAP + rank

    acc[...] = jnp.full_like(acc, -1.0)

    for i in range(4):
        loading(i).wait()

    def dispatch(h):
        base = h * PAIR
        pick = position == base + lax.broadcasted_iota(jnp.int32, (PAIR, rows), 0)
        chosen = jnp.where(pick, 1.0, 0.0)
        filled = jnp.sum(chosen, axis=1, keepdims=True)
        wide = jnp.dot(chosen.astype(jnp.bfloat16), emb[...], preferred_element_type=jnp.float32)
        total = jnp.sum(wide * wide, axis=1, keepdims=True)
        wide = wide * (1.0 / jnp.sqrt(total + 1e-06))
        lane = lax.broadcasted_iota(jnp.int32, (PAIR, LANES), 1)
        mark = jnp.where((lane == 0) & (filled == 0.0), EMPTY, 0.0)
        send[pl.ds(base, PAIR), :LANES] = (wide[:, :LANES] + mark).astype(jnp.bfloat16)
        send[pl.ds(base, PAIR), LANES:] = wide[:, LANES:].astype(jnp.bfloat16)

    def outgoing(d, g):
        src = pl.ds(g * GRP + d * CAP, CAP)
        dst = pl.ds((g // 2) * BOTH + (g % 2) * GRP + d * CAP, CAP)
        return pltpu.make_async_remote_copy(
            src_ref=send.at[src], dst_ref=pool.at[dst], send_sem=send_sem, recv_sem=recv_sem.at[g],
            device_id=ahead(d, g), device_id_type=MESH,
        )

    def send_near(h):
        for d, g in NEAR:
            if g // 2 == h:
                outgoing(d, g).start()

    for h in range(EARLY):
        dispatch(h)

    @pl.when(core == 0)
    def _():
        pl.semaphore_wait(barrier, 2 * len(NEAR) + 1)
        pl.semaphore_signal(near_sem, inc=1, device_id=sibling, device_id_type=MESH)

    @pl.when(core == 1)
    def _():
        pl.semaphore_wait(near_sem, 1)

    for h in range(EARLY):
        send_near(h)
    for h in range(EARLY, PAIRS):
        dispatch(h)
        send_near(h)

    own_src = pl.ds((PLANE - 1) * GRP, CAP)
    own_dst = pl.ds((PAIRS - 1) * BOTH + GRP, CAP)
    pltpu.make_async_copy(send.at[own_src], pool.at[own_dst], recv_sem.at[PLANE - 1]).start()

    @pl.when(core == 1)
    def _():
        pl.semaphore_wait(barrier, 2 * len(FAR) + 1)
        pl.semaphore_signal(far_sem, inc=1, device_id=sibling, device_id_type=MESH)

    @pl.when(core == 0)
    def _():
        pl.semaphore_wait(far_sem, 1)

    for d, g in FAR:
        outgoing(d, g).start()

    def mine(h, odd):
        return pl.ds(pl.multiple_of(h * BOTH + odd * GRP, GRP), GRP)

    def theirs(h, odd):
        return pl.ds(pl.multiple_of(h * BOTH + PAIR + odd * GRP, GRP), GRP)

    def forward(h, odd):
        g = 2 * h + odd
        return pltpu.make_async_remote_copy(
            src_ref=pool.at[mine(h, odd)], dst_ref=pool.at[theirs(h, odd)],
            send_sem=fwd_send, recv_sem=fwd_recv.at[g], device_id=sibling, device_id_type=MESH,
        )

    def arrive(h, odd):
        at = mine(h, odd)
        pltpu.make_async_copy(pool.at[at], pool.at[at], recv_sem.at[2 * h + odd]).wait()

    def meet(other, i, same):
        own = pool[pl.ds(pl.multiple_of(i * BOTH, BOTH), PAIR), :]
        score = lax.dot_general(other, own, (((1,), (1,)), ((), ())), preferred_element_type=jnp.float32)
        score = score + jnp.where(other[:, 0:1].astype(jnp.float32) > 2.0, LOW, 0.0)
        if same:
            one = lax.broadcasted_iota(jnp.int32, score.shape, 0)
            two = lax.broadcasted_iota(jnp.int32, score.shape, 1)
            score = jnp.where(one == two, LOW, score)
        best = jnp.max(score.reshape(score.shape[0] // 8, 8, PAIR), axis=0)
        at = pl.ds(pl.multiple_of(i * PAIR, PAIR), PAIR)
        acc[:, at] = jnp.maximum(acc[:, at], best)

    def whole(h):
        return pool[pl.ds(pl.multiple_of(h * BOTH, BOTH), BOTH), :]

    def newest(h, odd):
        return jnp.concatenate([pool[mine(h, odd), :], pool[theirs(h, odd), :]], axis=0)

    def cross(h, i):
        meet(whole(i), h, False)
        meet(whole(h), i, False)

    @pl.loop(0, PAIRS - 1)
    def _(h):
        for odd in range(2):
            arrive(h, odd)
            forward(h, odd).start()
        for odd in range(2):
            forward(h, odd).wait_recv()

        @pl.loop(0, h // 2)
        def _(k):
            cross(h, 2 * k)
            cross(h, 2 * k + 1)

        @pl.loop(0, h % 2)
        def _(k):
            cross(h, h - 1)

        meet(whole(h), h, True)

    last = PAIRS - 1

    def returning(d, g):
        return pltpu.make_async_remote_copy(
            src_ref=res.at[g], dst_ref=back.at[g * NZ + d], send_sem=ret_send, recv_sem=ret_recv,
            device_id=behind(d, g), device_id_type=MESH,
        )

    def finish(i):
        best = jnp.max(acc[:, i * PAIR:(i + 1) * PAIR], axis=0, keepdims=True)
        for odd in range(2):
            g = 2 * i + odd
            res[g] = best[:, odd * LANES:(odd + 1) * LANES]
            for d in range(NZ):
                if g == PLANE - 1 and d == 0:
                    pltpu.make_async_copy(res.at[g], back.at[g * NZ], ret_recv).start()
                else:
                    returning(d, g).start()

    arrive(last, 0)
    forward(last, 0).start()
    forward(last, 0).wait_recv()

    for i in range(last):
        meet(newest(last, 0), i, False)
    arrive(last, 1)
    forward(last, 1).start()
    for j in range(last):
        meet(whole(j), last, False)
    forward(last, 1).wait_recv()
    for i in range(last):
        meet(newest(last, 1), i, False)
        finish(i)
    meet(whole(last), last, True)
    finish(last)

    pltpu.make_async_copy(back, back, ret_recv).wait()

    got = back[...].reshape(CHIPS, LANES)
    high = got.astype(jnp.bfloat16)
    rest = got - high.astype(jnp.float32)
    middle = rest.astype(jnp.bfloat16)
    low = (rest - middle.astype(jnp.float32)).astype(jnp.bfloat16)
    spread = jnp.zeros((LANES, rows), jnp.float32)
    for part in (high, middle, low):
        spread += lax.dot_general(
            part, onehot[...], (((0,), (0,)), ((), ())), preferred_element_type=jnp.float32
        )
    place = far_z * CAP + rank
    chosen = place == lax.broadcasted_iota(jnp.int32, (LANES, rows), 0)
    out_ref[...] = jnp.sum(jnp.where(chosen, spread, 0.0), axis=0, keepdims=True)

    sent = pl.ds(CAP, (CHIPS - 1) * CAP)
    pltpu.make_async_copy(send.at[sent], send.at[sent], send_sem).wait()
    half = pl.ds(0, PLANE * GRP)
    pltpu.make_async_copy(pool.at[half], pool.at[half], fwd_send).wait()
    others = pl.ds(0, CHIPS - 1)
    pltpu.make_async_copy(back.at[others], back.at[others], ret_send).wait()


def on_device(embeddings, cluster_of):
    rows, features = embeddings.shape
    slots = CHIPS * CAP
    nearest = pl.pallas_call(
        kernel,
        out_shape=jax.ShapeDtypeStruct((1, rows), jnp.float32),
        in_specs=[pl.BlockSpec(memory_space=pltpu.HBM), pl.BlockSpec(memory_space=pltpu.VMEM)],
        out_specs=pl.BlockSpec(memory_space=pltpu.VMEM),
        scratch_shapes=[
            pltpu.VMEM((rows, features), jnp.bfloat16),
            pltpu.VMEM((slots, features), jnp.bfloat16),
            pltpu.VMEM((2 * slots, features), jnp.bfloat16),
            pltpu.VMEM((8, slots), jnp.float32),
            pltpu.VMEM((PLANE, 1, LANES), jnp.float32),
            pltpu.VMEM((CHIPS, 1, LANES), jnp.float32),
            pltpu.VMEM((CHIPS, rows), jnp.bfloat16),
            pltpu.SemaphoreType.DMA((4,)),
            pltpu.SemaphoreType.REGULAR,
            pltpu.SemaphoreType.REGULAR,
            pltpu.SemaphoreType.DMA,
            pltpu.SemaphoreType.DMA((PLANE,)),
            pltpu.SemaphoreType.DMA,
            pltpu.SemaphoreType.DMA((PLANE,)),
            pltpu.SemaphoreType.DMA,
            pltpu.SemaphoreType.DMA,
        ],
        compiler_params=pltpu.CompilerParams(
            collective_id=0, has_side_effects=True, vmem_limit_bytes=53 << 20
        ),
        cost_estimate=pl.CostEstimate(
            flops=2 * slots * 2 * slots * features, bytes_accessed=2 * rows * features, transcendentals=0
        ),
    )(embeddings, cluster_of.reshape(1, rows))
    return nearest.reshape(rows)


def solution(mesh):
    return jax.shard_map(
        on_device,
        mesh=mesh,
        in_specs=(P(("dp", "group"), None), P(("dp", "group"), None)),
        out_specs=P(("dp", "group")),
        check_vma=False,
    )
```

```python
import jax
import jax.numpy as jnp
from jax import lax
from jax.experimental import pallas as pl
from jax.experimental.pallas import tpu as pltpu
from jax.sharding import PartitionSpec as P

MESH = pl.DeviceIdType.MESH
NZ, NX, NY = 8, 4, 4
PLANE = NX * NY
CHIPS = NZ * PLANE
CAP = 16
GRP = NZ * CAP
PAIR = 2 * GRP
BOTH = 2 * PAIR
PAIRS = PLANE // 2
EARLY = 2
LOOPED = 6
FAR_FIRST = (2, 0, 3, 4, 1, 5, 6)
EMPTY = 4.0
LOW = -1e30
LANES = 128


OFFSETS = [(d, g) for g in range(PLANE) for d in range(NZ) if (d, g) != (0, PLANE - 1)]


def kernel(
    emb_hbm, lab_ref, out_ref,
    emb, send, pool, acc, res, back, onehot,
    emb_sem, send_sem, recv_sem, fwd_send, fwd_recv, ret_send, ret_recv,
):
    dp = lax.axis_index("dp")
    y = lax.axis_index("group")
    z, x, core = dp // (2 * NX), (dp // 2) % NX, dp % 2
    rows = emb.shape[0]
    quarter = rows // 4

    def loading(i):
        at = pl.ds(i * quarter, quarter)
        return pltpu.make_async_copy(emb_hbm.at[at], emb.at[at], emb_sem.at[i])

    for i in range(4):
        loading(i).start()

    z_ahead = [((z + d) % NZ) * (2 * NX) + core for d in range(NZ)]
    z_behind = [((z + NZ - d) % NZ) * (2 * NX) + core for d in range(NZ)]

    x_ahead = [((x + d) % NX) * 2 for d in range(NX)]
    y_ahead = [(y + d) % NY for d in range(NY)]

    def ahead(d, g):
        p = PLANE - 1 - g
        return (z_ahead[d] + x_ahead[p // NY], y_ahead[p % NY])

    def behind(d, g):
        p = PLANE - 1 - g
        return (z_behind[d] + x_ahead[-(p // NY)], y_ahead[-(p % NY)])

    sibling = ((z * NX + x) * 2 + 1 - core, y)

    barrier = pltpu.get_barrier_semaphore()

    for offset in OFFSETS:
        pl.semaphore_signal(barrier, inc=1, device_id=ahead(*offset), device_id_type=MESH)
    pl.semaphore_signal(barrier, inc=1, device_id=sibling, device_id_type=MESH)

    label = lab_ref[...]
    far_z = (label % NZ - z + NZ) % NZ
    far_x = (label // PLANE // 2 - x + NX) % NX
    far_y = ((label // NZ) % NY - y + NY) % NY
    chip = (PLANE - 1 - far_x * NY - far_y) * NZ + far_z
    hot = chip == lax.broadcasted_iota(jnp.int32, (CHIPS, rows), 0)
    ones = hot.astype(jnp.bfloat16)
    onehot[...] = ones
    row = lax.broadcasted_iota(jnp.int32, (LANES, 2 * LANES), 0)
    col = lax.broadcasted_iota(jnp.int32, (LANES, 2 * LANES), 1)
    before = ((row < col) | (col >= LANES)).astype(jnp.bfloat16)
    ranks = []
    carry = jnp.zeros((CHIPS, LANES), jnp.float32)
    for t in range(rows // LANES):
        at = slice(t * LANES, (t + 1) * LANES)
        both = jnp.dot(ones[:, at], before, preferred_element_type=jnp.float32)
        earlier = jnp.where(hot[:, at], both[:, :LANES] + carry, 0.0)
        carry = carry + both[:, LANES:]
        ranks.append(jnp.sum(earlier, axis=0, keepdims=True))
    rank = jnp.concatenate(ranks, axis=1).astype(jnp.int32)
    position = chip * CAP + rank

    acc[...] = jnp.full_like(acc, -1.0)

    for i in range(4):
        loading(i).wait()

    def dispatch(h):
        base = h * PAIR
        pick = position == base + lax.broadcasted_iota(jnp.int32, (PAIR, rows), 0)
        chosen = jnp.where(pick, 1.0, 0.0)
        filled = jnp.sum(chosen, axis=1, keepdims=True)
        wide = jnp.dot(chosen.astype(jnp.bfloat16), emb[...], preferred_element_type=jnp.float32)
        total = jnp.sum(wide * wide, axis=1, keepdims=True)
        wide = wide * (1.0 / jnp.sqrt(total + 1e-06))
        lane = lax.broadcasted_iota(jnp.int32, (PAIR, LANES), 1)
        mark = jnp.where((lane == 0) & (filled == 0.0), EMPTY, 0.0)
        send[pl.ds(base, PAIR), :LANES] = (wide[:, :LANES] + mark).astype(jnp.bfloat16)
        send[pl.ds(base, PAIR), LANES:] = wide[:, LANES:].astype(jnp.bfloat16)

    def outgoing(d, g):
        src = pl.ds(g * GRP + d * CAP, CAP)
        dst = pl.ds((g // 2) * BOTH + (g % 2) * GRP + d * CAP, CAP)
        return pltpu.make_async_remote_copy(
            src_ref=send.at[src], dst_ref=pool.at[dst], send_sem=send_sem, recv_sem=recv_sem.at[g],
            device_id=ahead(d, g), device_id_type=MESH,
        )

    for h in range(EARLY):
        dispatch(h)

    pl.semaphore_wait(barrier, CHIPS)

    for h in range(PAIRS):
        if h >= EARLY:
            dispatch(h)
        if h == PAIRS - 1:
            own_src = pl.ds((PLANE - 1) * GRP, CAP)
            own_dst = pl.ds((PAIRS - 1) * BOTH + GRP, CAP)
            pltpu.make_async_copy(send.at[own_src], pool.at[own_dst], recv_sem.at[PLANE - 1]).start()
        for d, g in OFFSETS:
            if g // 2 == h:
                outgoing(d, g).start()

    def mine(h, odd):
        return pl.ds(pl.multiple_of(h * BOTH + odd * GRP, GRP), GRP)

    def theirs(h, odd):
        return pl.ds(pl.multiple_of(h * BOTH + PAIR + odd * GRP, GRP), GRP)

    def forward(h, odd):
        g = 2 * h + odd
        return pltpu.make_async_remote_copy(
            src_ref=pool.at[mine(h, odd)], dst_ref=pool.at[theirs(h, odd)],
            send_sem=fwd_send, recv_sem=fwd_recv.at[g], device_id=sibling, device_id_type=MESH,
        )

    def arrive(h, odd):
        at = mine(h, odd)
        pltpu.make_async_copy(pool.at[at], pool.at[at], recv_sem.at[2 * h + odd]).wait()

    def meet(other, i, same):
        own = pool[pl.ds(pl.multiple_of(i * BOTH, BOTH), PAIR), :]
        score = lax.dot_general(other, own, (((1,), (1,)), ((), ())), preferred_element_type=jnp.float32)
        score = score + jnp.where(other[:, 0:1].astype(jnp.float32) > 2.0, LOW, 0.0)
        if same:
            one = lax.broadcasted_iota(jnp.int32, score.shape, 0)
            two = lax.broadcasted_iota(jnp.int32, score.shape, 1)
            score = jnp.where(one == two, LOW, score)
        best = jnp.max(score.reshape(score.shape[0] // 8, 8, PAIR), axis=0)
        at = pl.ds(pl.multiple_of(i * PAIR, PAIR), PAIR)
        acc[:, at] = jnp.maximum(acc[:, at], best)

    def whole(h):
        return pool[pl.ds(pl.multiple_of(h * BOTH, BOTH), BOTH), :]

    def newest(h, odd):
        return jnp.concatenate([pool[mine(h, odd), :], pool[theirs(h, odd), :]], axis=0)

    def cross(h, i):
        meet(whole(i), h, False)
        meet(whole(h), i, False)

    @pl.loop(0, LOOPED)
    def _(h):
        for odd in range(2):
            arrive(h, odd)
            forward(h, odd).start()
        for odd in range(2):
            forward(h, odd).wait_recv()

        @pl.loop(0, h // 2)
        def _(k):
            cross(h, 2 * k)
            cross(h, 2 * k + 1)

        @pl.loop(0, h % 2)
        def _(k):
            cross(h, h - 1)

        meet(whole(h), h, True)

    last = PAIRS - 1

    def returning(d, g):
        return pltpu.make_async_remote_copy(
            src_ref=res.at[g], dst_ref=back.at[g * NZ + d], send_sem=ret_send, recv_sem=ret_recv,
            device_id=behind(d, g), device_id_type=MESH,
        )

    def finish(i):
        best = jnp.max(acc[:, i * PAIR:(i + 1) * PAIR], axis=0, keepdims=True)
        for odd in range(2):
            g = 2 * i + odd
            res[g] = best[:, odd * LANES:(odd + 1) * LANES]
            for d in range(NZ):
                if g == PLANE - 1 and d == 0:
                    pltpu.make_async_copy(res.at[g], back.at[g * NZ], ret_recv).start()
                else:
                    returning(d, g).start()

    def step(h, odd, then):
        arrive(h, odd)
        forward(h, odd).start()
        if odd:
            for j in range(h):
                meet(whole(j), h, False)
        forward(h, odd).wait_recv()
        for i in FAR_FIRST:
            if i < h:
                meet(newest(h, odd), i, False)
                then(i)
        if odd:
            meet(whole(h), h, True)
            then(h)

    for h in range(LOOPED, last):
        step(h, 0, lambda i: None)
        step(h, 1, lambda i: None)
    step(last, 0, lambda i: None)
    step(last, 1, finish)

    pltpu.make_async_copy(back, back, ret_recv).wait()

    got = back[...].reshape(CHIPS, LANES)
    high = got.astype(jnp.bfloat16)
    rest = got - high.astype(jnp.float32)
    low = rest.astype(jnp.bfloat16)
    spread = jnp.zeros((LANES, rows), jnp.float32)
    for part in (high, low):
        spread += lax.dot_general(
            part, onehot[...], (((0,), (0,)), ((), ())), preferred_element_type=jnp.float32
        )
    place = far_z * CAP + rank
    chosen = place == lax.broadcasted_iota(jnp.int32, (LANES, rows), 0)
    out_ref[...] = jnp.sum(jnp.where(chosen, spread, 0.0), axis=0, keepdims=True)

    sent = pl.ds(CAP, (CHIPS - 1) * CAP)
    pltpu.make_async_copy(send.at[sent], send.at[sent], send_sem).wait()
    half = pl.ds(0, PLANE * GRP)
    pltpu.make_async_copy(pool.at[half], pool.at[half], fwd_send).wait()
    others = pl.ds(0, CHIPS - 1)
    pltpu.make_async_copy(back.at[others], back.at[others], ret_send).wait()


def on_device(embeddings, cluster_of):
    rows, features = embeddings.shape
    slots = CHIPS * CAP
    nearest = pl.pallas_call(
        kernel,
        out_shape=jax.ShapeDtypeStruct((1, rows), jnp.float32),
        in_specs=[pl.BlockSpec(memory_space=pltpu.HBM), pl.BlockSpec(memory_space=pltpu.VMEM)],
        out_specs=pl.BlockSpec(memory_space=pltpu.VMEM),
        scratch_shapes=[
            pltpu.VMEM((rows, features), jnp.bfloat16),
            pltpu.VMEM((slots, features), jnp.bfloat16),
            pltpu.VMEM((2 * slots, features), jnp.bfloat16),
            pltpu.VMEM((8, slots), jnp.float32),
            pltpu.VMEM((PLANE, 1, LANES), jnp.float32),
            pltpu.VMEM((CHIPS, 1, LANES), jnp.float32),
            pltpu.VMEM((CHIPS, rows), jnp.bfloat16),
            pltpu.SemaphoreType.DMA((4,)),
            pltpu.SemaphoreType.DMA,
            pltpu.SemaphoreType.DMA((PLANE,)),
            pltpu.SemaphoreType.DMA,
            pltpu.SemaphoreType.DMA((PLANE,)),
            pltpu.SemaphoreType.DMA,
            pltpu.SemaphoreType.DMA,
        ],
        compiler_params=pltpu.CompilerParams(
            collective_id=0, has_side_effects=True, vmem_limit_bytes=53 << 20
        ),
        cost_estimate=pl.CostEstimate(
            flops=2 * slots * 2 * slots * features, bytes_accessed=2 * rows * features, transcendentals=0
        ),
    )(embeddings, cluster_of.reshape(1, rows))
    return nearest.reshape(rows)


def solution(mesh):
    return jax.shard_map(
        on_device,
        mesh=mesh,
        in_specs=(P(("dp", "group"), None), P(("dp", "group"), None)),
        out_specs=P(("dp", "group")),
        check_vma=False,
    )
```

```python
import jax
import jax.numpy as jnp
from jax import lax
from jax.experimental import pallas as pl
from jax.experimental.pallas import tpu as pltpu
from jax.sharding import PartitionSpec as P

MESH = pl.DeviceIdType.MESH
NZ, NX, NY = 8, 4, 4
PLANE = NX * NY
CHIPS = NZ * PLANE
CAP = 16
GRP = NZ * CAP
PAIR = 2 * GRP
BOTH = 2 * PAIR
PAIRS = PLANE // 2
EARLY = 2
LOOPED = 6
BESIDE = 4
EMPTY = 4.0
LOW = -1e30
LANES = 128


def steps(r):
    p = PLANE - 1 - r // NZ
    return r % NZ, p // NY, p % NY


def hops(r):
    return sum(min(a, n - a) for a, n in zip(steps(r), (NZ, NX, NY)))


def arrange():
    by_hops = sorted(range(CHIPS), key=lambda r: (hops(r), -r))
    at = list(range(CHIPS))
    for g, chosen in ((PLANE - 1, by_hops[:NZ]), (PLANE - 2, by_hops[NZ:2 * NZ])):
        slots = range(g * NZ, (g + 1) * NZ)
        coming = [r for r in chosen if at.index(r) not in slots]
        for s in slots:
            if at[s] not in chosen:
                t = at.index(coming.pop())
                at[s], at[t] = at[t], at[s]
    return at


AT = arrange()
SELF = AT.index((PLANE - 1) * NZ)
OTHERS = [s for s in range(CHIPS) if s != SELF]
FAR_FIRST = sorted(range(PAIRS - 1), key=lambda i: -max(hops(r) for r in AT[2 * NZ * i:2 * NZ * (i + 1)]))


def kernel(
    emb_hbm, lab_hbm, out_ref,
    emb, lab, send, pool, acc, res, back, onehot,
    emb_sem, lab_sem, send_sem, recv_sem, fwd_send, fwd_recv, ret_send, ret_recv,
):
    dp = lax.axis_index("dp")
    y = lax.axis_index("group")
    z, x, core = dp // (2 * NX), (dp // 2) % NX, dp % 2
    rows = emb.shape[0]
    quarter = rows // 4

    def loading(i):
        at = pl.ds(i * quarter, quarter)
        return pltpu.make_async_copy(emb_hbm.at[at], emb.at[at], emb_sem.at[i])

    labels = pltpu.make_async_copy(lab_hbm, lab, lab_sem)
    labels.start()
    for i in range(4):
        loading(i).start()

    z_ahead = [((z + d) % NZ) * (2 * NX) + core for d in range(NZ)]
    z_behind = [((z + NZ - d) % NZ) * (2 * NX) + core for d in range(NZ)]

    x_ahead = [((x + d) % NX) * 2 for d in range(NX)]
    y_ahead = [(y + d) % NY for d in range(NY)]

    def ahead(s):
        dz, dx, dy = steps(AT[s])
        return (z_ahead[dz] + x_ahead[dx], y_ahead[dy])

    def behind(s):
        dz, dx, dy = steps(AT[s])
        return (z_behind[dz] + x_ahead[-dx], y_ahead[-dy])

    sibling = ((z * NX + x) * 2 + 1 - core, y)

    barrier = pltpu.get_barrier_semaphore()

    for s in OTHERS:
        pl.semaphore_signal(barrier, inc=1, device_id=ahead(s), device_id_type=MESH)
    pl.semaphore_signal(barrier, inc=1, device_id=sibling, device_id_type=MESH)

    labels.wait()
    label = lab[...]
    far_z = (label % NZ - z + NZ) % NZ
    far_x = (label // PLANE // 2 - x + NX) % NX
    far_y = ((label // NZ) % NY - y + NY) % NY
    offset = (PLANE - 1 - far_x * NY - far_y) * NZ + far_z
    chip = offset
    for s, r in enumerate(AT):
        if s != r:
            chip = jnp.where(offset == r, s, chip)
    hot = chip == lax.broadcasted_iota(jnp.int32, (CHIPS, rows), 0)
    ones = hot.astype(jnp.bfloat16)
    onehot[...] = ones
    row = lax.broadcasted_iota(jnp.int32, (LANES, 2 * LANES), 0)
    col = lax.broadcasted_iota(jnp.int32, (LANES, 2 * LANES), 1)
    before = ((row < col) | (col >= LANES)).astype(jnp.bfloat16)
    ranks = []
    carry = jnp.zeros((CHIPS, LANES), jnp.float32)
    for t in range(rows // LANES):
        at = slice(t * LANES, (t + 1) * LANES)
        both = jnp.dot(ones[:, at], before, preferred_element_type=jnp.float32)
        earlier = jnp.where(hot[:, at], both[:, :LANES] + carry, 0.0)
        carry = carry + both[:, LANES:]
        ranks.append(jnp.sum(earlier, axis=0, keepdims=True))
    rank = jnp.concatenate(ranks, axis=1).astype(jnp.int32)
    position = chip * CAP + rank

    acc[...] = jnp.full_like(acc, -1.0)

    for i in range(4):
        loading(i).wait()

    def dispatch(h):
        base = h * PAIR
        pick = position == base + lax.broadcasted_iota(jnp.int32, (PAIR, rows), 0)
        chosen = jnp.where(pick, 1.0, 0.0)
        filled = jnp.sum(chosen, axis=1, keepdims=True)
        wide = jnp.dot(chosen.astype(jnp.bfloat16), emb[...], preferred_element_type=jnp.float32)
        total = jnp.sum(wide * wide, axis=1, keepdims=True)
        wide = wide * (1.0 / jnp.sqrt(total + 1e-06))
        lane = lax.broadcasted_iota(jnp.int32, (PAIR, LANES), 1)
        mark = jnp.where((lane == 0) & (filled == 0.0), EMPTY, 0.0)
        send[pl.ds(base, PAIR), :LANES] = (wide[:, :LANES] + mark).astype(jnp.bfloat16)
        send[pl.ds(base, PAIR), LANES:] = wide[:, LANES:].astype(jnp.bfloat16)

    def landing(s):
        return pl.ds((s // (2 * NZ)) * BOTH + s % (2 * NZ) * CAP, CAP)

    def outgoing(s):
        src, dst = pl.ds(s * CAP, CAP), landing(s)
        return pltpu.make_async_remote_copy(
            src_ref=send.at[src], dst_ref=pool.at[dst], send_sem=send_sem, recv_sem=recv_sem.at[s // NZ],
            device_id=ahead(s), device_id_type=MESH,
        )

    for h in range(EARLY):
        dispatch(h)

    pl.semaphore_wait(barrier, CHIPS)

    for h in range(PAIRS):
        if h >= EARLY:
            dispatch(h)
        for s in range(h * 2 * NZ, (h + 1) * 2 * NZ):
            if s == SELF:
                pltpu.make_async_copy(
                    send.at[pl.ds(s * CAP, CAP)], pool.at[landing(s)], recv_sem.at[s // NZ]
                ).start()
            else:
                outgoing(s).start()

    def mine(h, odd):
        return pl.ds(pl.multiple_of(h * BOTH + odd * GRP, GRP), GRP)

    def theirs(h, odd):
        return pl.ds(pl.multiple_of(h * BOTH + PAIR + odd * GRP, GRP), GRP)

    def forward(h, odd):
        g = 2 * h + odd
        return pltpu.make_async_remote_copy(
            src_ref=pool.at[mine(h, odd)], dst_ref=pool.at[theirs(h, odd)],
            send_sem=fwd_send, recv_sem=fwd_recv.at[g], device_id=sibling, device_id_type=MESH,
        )

    def arrive(h, odd):
        at = mine(h, odd)
        pltpu.make_async_copy(pool.at[at], pool.at[at], recv_sem.at[2 * h + odd]).wait()

    def meet(other, i, same):
        own = pool[pl.ds(pl.multiple_of(i * BOTH, BOTH), PAIR), :]
        score = lax.dot_general(other, own, (((1,), (1,)), ((), ())), preferred_element_type=jnp.float32)
        score = score + jnp.where(other[:, 0:1].astype(jnp.float32) > 2.0, LOW, 0.0)
        if same:
            one = lax.broadcasted_iota(jnp.int32, score.shape, 0)
            two = lax.broadcasted_iota(jnp.int32, score.shape, 1)
            score = jnp.where(one == two, LOW, score)
        best = jnp.max(score.reshape(score.shape[0] // 8, 8, PAIR), axis=0)
        at = pl.ds(pl.multiple_of(i * PAIR, PAIR), PAIR)
        acc[:, at] = jnp.maximum(acc[:, at], best)

    def whole(h):
        return pool[pl.ds(pl.multiple_of(h * BOTH, BOTH), BOTH), :]

    def newest(h, odd):
        return jnp.concatenate([pool[mine(h, odd), :], pool[theirs(h, odd), :]], axis=0)

    def cross(h, i):
        meet(whole(i), h, False)
        meet(whole(h), i, False)

    @pl.loop(0, LOOPED)
    def _(h):
        for odd in range(2):
            arrive(h, odd)
            forward(h, odd).start()
        for odd in range(2):
            forward(h, odd).wait_recv()

        @pl.loop(0, h // 2)
        def _(k):
            cross(h, 2 * k)
            cross(h, 2 * k + 1)

        @pl.loop(0, h % 2)
        def _(k):
            cross(h, h - 1)

        meet(whole(h), h, True)

    last = PAIRS - 1

    def returning(s):
        return pltpu.make_async_remote_copy(
            src_ref=res.at[s // NZ], dst_ref=back.at[s], send_sem=ret_send, recv_sem=ret_recv,
            device_id=behind(s), device_id_type=MESH,
        )

    def finish(i):
        best = jnp.max(acc[:, i * PAIR:(i + 1) * PAIR], axis=0, keepdims=True)
        for odd in range(2):
            g = 2 * i + odd
            res[g] = best[:, odd * LANES:(odd + 1) * LANES]
            for s in range(g * NZ, (g + 1) * NZ):
                if s == SELF:
                    pltpu.make_async_copy(res.at[g], back.at[s], ret_recv).start()
                else:
                    returning(s).start()

    def step(h, odd, then):
        arrive(h, odd)
        forward(h, odd).start()
        if odd:
            for j in range(min(h, BESIDE)):
                meet(whole(j), h, False)
        forward(h, odd).wait_recv()
        for i in FAR_FIRST:
            if i < h:
                meet(newest(h, odd), i, False)
                then(i)
        if odd:
            for j in range(BESIDE, h):
                meet(whole(j), h, False)
            meet(whole(h), h, True)
            then(h)

    for h in range(LOOPED, last):
        step(h, 0, lambda i: None)
        step(h, 1, lambda i: None)
    step(last, 0, lambda i: None)
    step(last, 1, finish)

    pltpu.make_async_copy(back, back, ret_recv).wait()

    got = back[...].reshape(CHIPS, LANES)
    high = got.astype(jnp.bfloat16)
    rest = got - high.astype(jnp.float32)
    low = rest.astype(jnp.bfloat16)
    spread = jnp.zeros((LANES, rows), jnp.float32)
    for part in (high, low):
        spread += lax.dot_general(
            part, onehot[...], (((0,), (0,)), ((), ())), preferred_element_type=jnp.float32
        )
    place = (chip % NZ) * CAP + rank
    chosen = place == lax.broadcasted_iota(jnp.int32, (LANES, rows), 0)
    out_ref[...] = jnp.sum(jnp.where(chosen, spread, 0.0), axis=0, keepdims=True)

    sent = pl.ds(0, (CHIPS - 1) * CAP)
    pltpu.make_async_copy(send.at[sent], send.at[sent], send_sem).wait()
    half = pl.ds(0, PLANE * GRP)
    pltpu.make_async_copy(pool.at[half], pool.at[half], fwd_send).wait()
    others = pl.ds(0, CHIPS - 1)
    pltpu.make_async_copy(back.at[others], back.at[others], ret_send).wait()


def on_device(embeddings, cluster_of):
    rows, features = embeddings.shape
    slots = CHIPS * CAP
    nearest = pl.pallas_call(
        kernel,
        out_shape=jax.ShapeDtypeStruct((1, rows), jnp.float32),
        in_specs=[pl.BlockSpec(memory_space=pltpu.HBM)] * 2,
        out_specs=pl.BlockSpec(memory_space=pltpu.VMEM),
        scratch_shapes=[
            pltpu.VMEM((rows, features), jnp.bfloat16),
            pltpu.VMEM((1, rows), jnp.int32),
            pltpu.VMEM((slots, features), jnp.bfloat16),
            pltpu.VMEM((2 * slots, features), jnp.bfloat16),
            pltpu.VMEM((8, slots), jnp.float32),
            pltpu.VMEM((PLANE, 1, LANES), jnp.float32),
            pltpu.VMEM((CHIPS, 1, LANES), jnp.float32),
            pltpu.VMEM((CHIPS, rows), jnp.bfloat16),
            pltpu.SemaphoreType.DMA((4,)),
            pltpu.SemaphoreType.DMA,
            pltpu.SemaphoreType.DMA,
            pltpu.SemaphoreType.DMA((PLANE,)),
            pltpu.SemaphoreType.DMA,
            pltpu.SemaphoreType.DMA((PLANE,)),
            pltpu.SemaphoreType.DMA,
            pltpu.SemaphoreType.DMA,
        ],
        compiler_params=pltpu.CompilerParams(
            collective_id=0, has_side_effects=True, vmem_limit_bytes=55228 << 10
        ),
        cost_estimate=pl.CostEstimate(
            flops=2 * slots * 2 * slots * features, bytes_accessed=2 * rows * features, transcendentals=0
        ),
    )(embeddings, cluster_of.reshape(1, rows))
    return nearest.reshape(rows)


def solution(mesh):
    return jax.shard_map(
        on_device,
        mesh=mesh,
        in_specs=(P(("dp", "group"), None), P(("dp", "group"), None)),
        out_specs=P(("dp", "group")),
        check_vma=False,
    )
```

```python
import jax
import jax.numpy as jnp
from jax import lax
from jax.experimental import pallas as pl
from jax.experimental.pallas import tpu as pltpu
from jax.sharding import PartitionSpec as P

MESH = pl.DeviceIdType.MESH
NZ, NX, NY = 8, 4, 4
PLANE = NX * NY
CHIPS = NZ * PLANE
CAP = 16
GRP = NZ * CAP
PAIR = 2 * GRP
BOTH = 2 * PAIR
PAIRS = PLANE // 2
EARLY = 1
LOOPED = 6
BESIDE = 4
EMPTY = 4.0
LOW = -1e30
LANES = 128


def steps(r):
    p = PLANE - 1 - r // NZ
    return r % NZ, p // NY, p % NY


def hops(r):
    return sum(min(a, n - a) for a, n in zip(steps(r), (NZ, NX, NY)))


SELF = (PLANE - 1) * NZ
OTHERS = [s for s in range(CHIPS) if s != SELF]
FAR_FIRST = sorted(range(PAIRS - 1), key=lambda i: -max(hops(s) for s in range(2 * NZ * i, 2 * NZ * (i + 1))))


def kernel(
    emb_hbm, lab_hbm, out_ref,
    emb, lab, send, pool, acc, res, back, onehot,
    emb_sem, lab_sem, send_sem, recv_sem, fwd_send, fwd_recv, ret_send, ret_recv,
):
    dp = lax.axis_index("dp")
    y = lax.axis_index("group")
    z, x, core = dp // (2 * NX), (dp // 2) % NX, dp % 2
    rows = emb.shape[0]
    quarter = rows // 4

    def loading(i):
        at = pl.ds(i * quarter, quarter)
        return pltpu.make_async_copy(emb_hbm.at[at], emb.at[at], emb_sem.at[i])

    labels = pltpu.make_async_copy(lab_hbm, lab, lab_sem)
    labels.start()
    for i in range(4):
        loading(i).start()

    sign = 1 - 2 * core
    z_ahead = [((z + sign * d + NZ) % NZ) * (2 * NX) + core for d in range(NZ)]
    x_ahead = [((x + sign * d + NX) % NX) * 2 for d in range(NX)]
    y_ahead = [(y + sign * d + NY) % NY for d in range(NY)]

    def ahead(s):
        dz, dx, dy = steps(s)
        return (z_ahead[dz] + x_ahead[dx], y_ahead[dy])

    def behind(s):
        dz, dx, dy = steps(s)
        return (z_ahead[-dz] + x_ahead[-dx], y_ahead[-dy])

    sibling = ((z * NX + x) * 2 + 1 - core, y)

    barrier = pltpu.get_barrier_semaphore()

    for s in OTHERS:
        pl.semaphore_signal(barrier, inc=1, device_id=ahead(s), device_id_type=MESH)
    pl.semaphore_signal(barrier, inc=1, device_id=sibling, device_id_type=MESH)

    labels.wait()
    label = lab[...]
    far_z = (sign * (label % NZ - z) + NZ) % NZ
    far_x = (sign * (label // (NZ * NY) - x) + NX) % NX
    far_y = (sign * ((label // NZ) % NY - y) + NY) % NY
    chip = (PLANE - 1 - far_x * NY - far_y) * NZ + far_z
    hot = chip == lax.broadcasted_iota(jnp.int32, (CHIPS, rows), 0)
    ones = hot.astype(jnp.bfloat16)
    onehot[...] = ones
    row = lax.broadcasted_iota(jnp.int32, (LANES, 2 * LANES), 0)
    col = lax.broadcasted_iota(jnp.int32, (LANES, 2 * LANES), 1)
    before = ((row < col) | (col >= LANES)).astype(jnp.bfloat16)
    ranks = []
    carry = jnp.zeros((CHIPS, LANES), jnp.float32)
    for t in range(rows // LANES):
        at = slice(t * LANES, (t + 1) * LANES)
        both = jnp.dot(ones[:, at], before, preferred_element_type=jnp.float32)
        earlier = jnp.where(hot[:, at], both[:, :LANES] + carry, 0.0)
        carry = carry + both[:, LANES:]
        ranks.append(jnp.sum(earlier, axis=0, keepdims=True))
    rank = jnp.concatenate(ranks, axis=1).astype(jnp.int32)
    position = chip * CAP + rank

    acc[...] = jnp.full_like(acc, -1.0)

    for i in range(4):
        loading(i).wait()

    def dispatch(h):
        base = h * PAIR
        pick = position == base + lax.broadcasted_iota(jnp.int32, (PAIR, rows), 0)
        chosen = jnp.where(pick, 1.0, 0.0)
        filled = jnp.sum(chosen, axis=1, keepdims=True)
        wide = jnp.dot(chosen.astype(jnp.bfloat16), emb[...], preferred_element_type=jnp.float32)
        total = jnp.sum(wide * wide, axis=1, keepdims=True)
        wide = wide * (1.0 / jnp.sqrt(total + 1e-06))
        lane = lax.broadcasted_iota(jnp.int32, (PAIR, LANES), 1)
        mark = jnp.where((lane == 0) & (filled == 0.0), EMPTY, 0.0)
        send[pl.ds(base, PAIR), :LANES] = (wide[:, :LANES] + mark).astype(jnp.bfloat16)
        send[pl.ds(base, PAIR), LANES:] = wide[:, LANES:].astype(jnp.bfloat16)

    def landing(s):
        return pl.ds((s // (2 * NZ)) * BOTH + s % (2 * NZ) * CAP, CAP)

    def outgoing(s):
        src, dst = pl.ds(s * CAP, CAP), landing(s)
        return pltpu.make_async_remote_copy(
            src_ref=send.at[src], dst_ref=pool.at[dst], send_sem=send_sem, recv_sem=recv_sem.at[s // NZ],
            device_id=ahead(s), device_id_type=MESH,
        )

    for h in range(EARLY):
        dispatch(h)

    pl.semaphore_wait(barrier, CHIPS)

    for h in range(PAIRS):
        if h >= EARLY:
            dispatch(h)
        for s in range(h * 2 * NZ, (h + 1) * 2 * NZ):
            if s == SELF:
                pltpu.make_async_copy(
                    send.at[pl.ds(s * CAP, CAP)], pool.at[landing(s)], recv_sem.at[s // NZ]
                ).start()
            else:
                outgoing(s).start()

    def mine(h, odd):
        return pl.ds(pl.multiple_of(h * BOTH + odd * GRP, GRP), GRP)

    def theirs(h, odd):
        return pl.ds(pl.multiple_of(h * BOTH + PAIR + odd * GRP, GRP), GRP)

    def forward(h, odd):
        g = 2 * h + odd
        return pltpu.make_async_remote_copy(
            src_ref=pool.at[mine(h, odd)], dst_ref=pool.at[theirs(h, odd)],
            send_sem=fwd_send, recv_sem=fwd_recv.at[g], device_id=sibling, device_id_type=MESH,
        )

    def arrive(h, odd):
        at = mine(h, odd)
        pltpu.make_async_copy(pool.at[at], pool.at[at], recv_sem.at[2 * h + odd]).wait()

    def meet(other, i, same):
        own = pool[pl.ds(pl.multiple_of(i * BOTH, BOTH), PAIR), :]
        score = lax.dot_general(other, own, (((1,), (1,)), ((), ())), preferred_element_type=jnp.float32)
        score = score + jnp.where(other[:, 0:1].astype(jnp.float32) > 2.0, LOW, 0.0)
        if same:
            one = lax.broadcasted_iota(jnp.int32, score.shape, 0)
            two = lax.broadcasted_iota(jnp.int32, score.shape, 1)
            score = jnp.where(one == two, LOW, score)
        best = jnp.max(score.reshape(score.shape[0] // 8, 8, PAIR), axis=0)
        at = pl.ds(pl.multiple_of(i * PAIR, PAIR), PAIR)
        acc[:, at] = jnp.maximum(acc[:, at], best)

    def whole(h):
        return pool[pl.ds(pl.multiple_of(h * BOTH, BOTH), BOTH), :]

    def newest(h, odd):
        return jnp.concatenate([pool[mine(h, odd), :], pool[theirs(h, odd), :]], axis=0)

    def cross(h, i):
        meet(whole(i), h, False)
        meet(whole(h), i, False)

    @pl.loop(0, LOOPED)
    def _(h):
        for odd in range(2):
            arrive(h, odd)
            forward(h, odd).start()
        for odd in range(2):
            forward(h, odd).wait_recv()

        @pl.loop(0, h // 2)
        def _(k):
            cross(h, 2 * k)
            cross(h, 2 * k + 1)

        @pl.loop(0, h % 2)
        def _(k):
            cross(h, h - 1)

        meet(whole(h), h, True)

    last = PAIRS - 1

    def returning(s):
        return pltpu.make_async_remote_copy(
            src_ref=res.at[s // NZ], dst_ref=back.at[s], send_sem=ret_send, recv_sem=ret_recv,
            device_id=behind(s), device_id_type=MESH,
        )

    def finish(i):
        best = jnp.max(acc[:, i * PAIR:(i + 1) * PAIR], axis=0, keepdims=True)
        for odd in range(2):
            g = 2 * i + odd
            res[g] = best[:, odd * LANES:(odd + 1) * LANES]
            for s in range(g * NZ, (g + 1) * NZ):
                if s == SELF:
                    pltpu.make_async_copy(res.at[g], back.at[s], ret_recv).start()
                else:
                    returning(s).start()

    def step(h, odd, then):
        arrive(h, odd)
        forward(h, odd).start()
        if odd:
            for j in range(min(h, BESIDE)):
                meet(whole(j), h, False)
        forward(h, odd).wait_recv()
        for i in FAR_FIRST:
            if i < h:
                meet(newest(h, odd), i, False)
        for i in FAR_FIRST:
            if i < h:
                then(i)
        if odd:
            for j in range(BESIDE, h):
                meet(whole(j), h, False)
            meet(whole(h), h, True)
            then(h)

    for h in range(LOOPED, last):
        step(h, 0, lambda i: None)
        step(h, 1, lambda i: None)
    step(last, 0, lambda i: None)
    step(last, 1, finish)

    pltpu.make_async_copy(back, back, ret_recv).wait()

    got = back[...].reshape(CHIPS, LANES)
    high = got.astype(jnp.bfloat16)
    rest = got - high.astype(jnp.float32)
    low = rest.astype(jnp.bfloat16)
    spread = jnp.zeros((LANES, rows), jnp.float32)
    for part in (high, low):
        spread += lax.dot_general(
            part, onehot[...], (((0,), (0,)), ((), ())), preferred_element_type=jnp.float32
        )
    place = far_z * CAP + rank
    chosen = place == lax.broadcasted_iota(jnp.int32, (LANES, rows), 0)
    out_ref[...] = jnp.sum(jnp.where(chosen, spread, 0.0), axis=0, keepdims=True)

    sent = pl.ds(0, (CHIPS - 1) * CAP)
    pltpu.make_async_copy(send.at[sent], send.at[sent], send_sem).wait()
    half = pl.ds(0, PLANE * GRP)
    pltpu.make_async_copy(pool.at[half], pool.at[half], fwd_send).wait()
    others = pl.ds(0, CHIPS - 1)
    pltpu.make_async_copy(back.at[others], back.at[others], ret_send).wait()


def on_device(embeddings, cluster_of):
    rows, features = embeddings.shape
    slots = CHIPS * CAP
    nearest = pl.pallas_call(
        kernel,
        out_shape=jax.ShapeDtypeStruct((1, rows), jnp.float32),
        in_specs=[pl.BlockSpec(memory_space=pltpu.HBM)] * 2,
        out_specs=pl.BlockSpec(memory_space=pltpu.VMEM),
        scratch_shapes=[
            pltpu.VMEM((rows, features), jnp.bfloat16),
            pltpu.VMEM((1, rows), jnp.int32),
            pltpu.VMEM((slots, features), jnp.bfloat16),
            pltpu.VMEM((2 * slots, features), jnp.bfloat16),
            pltpu.VMEM((8, slots), jnp.float32),
            pltpu.VMEM((PLANE, 1, LANES), jnp.float32),
            pltpu.VMEM((CHIPS, 1, LANES), jnp.float32),
            pltpu.VMEM((CHIPS, rows), jnp.bfloat16),
            pltpu.SemaphoreType.DMA((4,)),
            pltpu.SemaphoreType.DMA,
            pltpu.SemaphoreType.DMA,
            pltpu.SemaphoreType.DMA((PLANE,)),
            pltpu.SemaphoreType.DMA,
            pltpu.SemaphoreType.DMA((PLANE,)),
            pltpu.SemaphoreType.DMA,
            pltpu.SemaphoreType.DMA,
        ],
        compiler_params=pltpu.CompilerParams(
            collective_id=0, has_side_effects=True, vmem_limit_bytes=55228 << 10
        ),
        cost_estimate=pl.CostEstimate(
            flops=2 * slots * 2 * slots * features, bytes_accessed=2 * rows * features, transcendentals=0
        ),
    )(embeddings, cluster_of.reshape(1, rows))
    return nearest.reshape(rows)


def solution(mesh):
    return jax.shard_map(
        on_device,
        mesh=mesh,
        in_specs=(P(("dp", "group"), None), P(("dp", "group"), None)),
        out_specs=P(("dp", "group")),
        check_vma=False,
    )
```

```python
import jax
import jax.numpy as jnp
from jax import lax
from jax.experimental import pallas as pl
from jax.experimental.pallas import tpu as pltpu
from jax.sharding import PartitionSpec as P

MESH = pl.DeviceIdType.MESH
NZ, NX, NY = 8, 4, 4
PLANE = NX * NY
CHIPS = NZ * PLANE
CAP = 16
GRP = NZ * CAP
PAIR = 2 * GRP
BOTH = 2 * PAIR
PAIRS = PLANE // 2
EARLY = 1
LOOPED = 6
BESIDE = 4
Z_ORDER = (4, 3, 5, 2, 6, 1, 7, 0)
EMPTY = 4.0
LOW = -1e30
LANES = 128


def steps(r):
    p = PLANE - 1 - r // NZ
    return r % NZ, p // NY, p % NY


def hops(r):
    return sum(min(a, n - a) for a, n in zip(steps(r), (NZ, NX, NY)))


SELF = (PLANE - 1) * NZ
OTHERS = [s for s in range(CHIPS) if s != SELF]
FAR_FIRST = sorted(range(PAIRS - 1), key=lambda i: -max(hops(s) for s in range(2 * NZ * i, 2 * NZ * (i + 1))))


def kernel(
    emb_hbm, lab_hbm, out_ref,
    emb, lab, send, pool, acc, res, back, onehot,
    emb_sem, lab_sem, send_sem, recv_sem, fwd_send, fwd_recv, ret_send, ret_recv,
):
    dp = lax.axis_index("dp")
    y = lax.axis_index("group")
    z, x, core = dp // (2 * NX), (dp // 2) % NX, dp % 2
    rows = emb.shape[0]
    quarter = rows // 4

    def loading(i):
        at = pl.ds(i * quarter, quarter)
        return pltpu.make_async_copy(emb_hbm.at[at], emb.at[at], emb_sem.at[i])

    labels = pltpu.make_async_copy(lab_hbm, lab, lab_sem)
    labels.start()
    for i in range(4):
        loading(i).start()

    sign = 1 - 2 * core
    z_ahead = [((z + sign * d + NZ) % NZ) * (2 * NX) + core for d in range(NZ)]
    x_ahead = [((x + sign * d + NX) % NX) * 2 for d in range(NX)]
    y_ahead = [(y + sign * d + NY) % NY for d in range(NY)]

    def ahead(s):
        dz, dx, dy = steps(s)
        return (z_ahead[dz] + x_ahead[dx], y_ahead[dy])

    def behind(s):
        dz, dx, dy = steps(s)
        return (z_ahead[-dz] + x_ahead[-dx], y_ahead[-dy])

    sibling = ((z * NX + x) * 2 + 1 - core, y)

    barrier = pltpu.get_barrier_semaphore()

    for s in OTHERS:
        pl.semaphore_signal(barrier, inc=1, device_id=ahead(s), device_id_type=MESH)
    pl.semaphore_signal(barrier, inc=1, device_id=sibling, device_id_type=MESH)

    labels.wait()
    label = lab[...]
    far_z = (sign * (label % NZ - z) + NZ) % NZ
    far_x = (sign * (label // (NZ * NY) - x) + NX) % NX
    far_y = (sign * ((label // NZ) % NY - y) + NY) % NY
    chip = (PLANE - 1 - far_x * NY - far_y) * NZ + far_z
    hot = chip == lax.broadcasted_iota(jnp.int32, (CHIPS, rows), 0)
    ones = hot.astype(jnp.bfloat16)
    row = lax.broadcasted_iota(jnp.int32, (LANES, 2 * LANES), 0)
    col = lax.broadcasted_iota(jnp.int32, (LANES, 2 * LANES), 1)
    before = ((row < col) | (col >= LANES)).astype(jnp.bfloat16)
    ranks = []
    carry = jnp.zeros((CHIPS, LANES), jnp.float32)
    for t in range(rows // LANES):
        at = slice(t * LANES, (t + 1) * LANES)
        both = jnp.dot(ones[:, at], before, preferred_element_type=jnp.float32)
        earlier = jnp.where(hot[:, at], both[:, :LANES] + carry, 0.0)
        carry = carry + both[:, LANES:]
        ranks.append(jnp.sum(earlier, axis=0, keepdims=True))
    rank = jnp.concatenate(ranks, axis=1).astype(jnp.int32)
    position = chip * CAP + rank

    acc[...] = jnp.full_like(acc, -1.0)

    for i in range(4):
        loading(i).wait()

    def dispatch(h):
        base = h * PAIR
        pick = position == base + lax.broadcasted_iota(jnp.int32, (PAIR, rows), 0)
        chosen = jnp.where(pick, 1.0, 0.0)
        filled = jnp.sum(chosen, axis=1, keepdims=True)
        wide = jnp.dot(chosen.astype(jnp.bfloat16), emb[...], preferred_element_type=jnp.float32)
        total = jnp.sum(wide * wide, axis=1, keepdims=True)
        wide = wide * (1.0 / jnp.sqrt(total + 1e-06))
        lane = lax.broadcasted_iota(jnp.int32, (PAIR, LANES), 1)
        mark = jnp.where((lane == 0) & (filled == 0.0), EMPTY, 0.0)
        send[pl.ds(base, PAIR), :LANES] = (wide[:, :LANES] + mark).astype(jnp.bfloat16)
        send[pl.ds(base, PAIR), LANES:] = wide[:, LANES:].astype(jnp.bfloat16)

    def landing(s):
        return pl.ds((s // (2 * NZ)) * BOTH + s % (2 * NZ) * CAP, CAP)

    def outgoing(s):
        src, dst = pl.ds(s * CAP, CAP), landing(s)
        return pltpu.make_async_remote_copy(
            src_ref=send.at[src], dst_ref=pool.at[dst], send_sem=send_sem, recv_sem=recv_sem.at[s // NZ],
            device_id=ahead(s), device_id_type=MESH,
        )

    for h in range(EARLY):
        dispatch(h)

    pl.semaphore_wait(barrier, CHIPS)

    for h in range(PAIRS):
        if h >= EARLY:
            dispatch(h)
        for s in [(2 * h + odd) * NZ + d for odd in range(2) for d in Z_ORDER]:
            if s == SELF:
                pltpu.make_async_copy(
                    send.at[pl.ds(s * CAP, CAP)], pool.at[landing(s)], recv_sem.at[s // NZ]
                ).start()
            else:
                outgoing(s).start()

    onehot[:CHIPS] = ones
    onehot[CHIPS:] = ones

    def mine(h, odd):
        return pl.ds(pl.multiple_of(h * BOTH + odd * GRP, GRP), GRP)

    def theirs(h, odd):
        return pl.ds(pl.multiple_of(h * BOTH + PAIR + odd * GRP, GRP), GRP)

    def forward(h, odd):
        g = 2 * h + odd
        return pltpu.make_async_remote_copy(
            src_ref=pool.at[mine(h, odd)], dst_ref=pool.at[theirs(h, odd)],
            send_sem=fwd_send, recv_sem=fwd_recv.at[g], device_id=sibling, device_id_type=MESH,
        )

    def arrive(h, odd):
        at = mine(h, odd)
        pltpu.make_async_copy(pool.at[at], pool.at[at], recv_sem.at[2 * h + odd]).wait()

    def meet(other, i, same):
        own = pool[pl.ds(pl.multiple_of(i * BOTH, BOTH), PAIR), :]
        score = lax.dot_general(other, own, (((1,), (1,)), ((), ())), preferred_element_type=jnp.float32)
        score = score + jnp.where(other[:, 0:1].astype(jnp.float32) > 2.0, LOW, 0.0)
        if same:
            one = lax.broadcasted_iota(jnp.int32, score.shape, 0)
            two = lax.broadcasted_iota(jnp.int32, score.shape, 1)
            score = jnp.where(one == two, LOW, score)
        best = jnp.max(score.reshape(score.shape[0] // 8, 8, PAIR), axis=0)
        at = pl.ds(pl.multiple_of(i * PAIR, PAIR), PAIR)
        acc[:, at] = jnp.maximum(acc[:, at], best)

    def whole(h):
        return pool[pl.ds(pl.multiple_of(h * BOTH, BOTH), BOTH), :]

    def newest(h, odd):
        return jnp.concatenate([pool[mine(h, odd), :], pool[theirs(h, odd), :]], axis=0)

    def cross(h, i):
        meet(whole(i), h, False)
        meet(whole(h), i, False)

    @pl.loop(0, LOOPED)
    def _(h):
        for odd in range(2):
            arrive(h, odd)
            forward(h, odd).start()
        for odd in range(2):
            forward(h, odd).wait_recv()

        @pl.loop(0, h // 2)
        def _(k):
            cross(h, 2 * k)
            cross(h, 2 * k + 1)

        @pl.loop(0, h % 2)
        def _(k):
            cross(h, h - 1)

        meet(whole(h), h, True)

    last = PAIRS - 1

    def returning(s):
        return pltpu.make_async_remote_copy(
            src_ref=res.at[s // NZ], dst_ref=back.at[s], send_sem=ret_send, recv_sem=ret_recv,
            device_id=behind(s), device_id_type=MESH,
        )

    def finish(i):
        best = jnp.max(acc[:, i * PAIR:(i + 1) * PAIR], axis=0, keepdims=True)
        for odd in range(2):
            g = 2 * i + odd
            res[g] = best[:, odd * LANES:(odd + 1) * LANES]
            for s in range(g * NZ, (g + 1) * NZ):
                if s == SELF:
                    pltpu.make_async_copy(res.at[g], back.at[s], ret_recv).start()
                else:
                    returning(s).start()

    def step(h, odd, then):
        arrive(h, odd)
        forward(h, odd).start()
        if odd:
            for j in range(min(h, BESIDE)):
                meet(whole(j), h, False)
        forward(h, odd).wait_recv()
        for i in FAR_FIRST:
            if i < h:
                meet(newest(h, odd), i, False)
        for i in FAR_FIRST:
            if i < h:
                then(i)
        if odd:
            for j in range(BESIDE, h):
                meet(whole(j), h, False)
            meet(whole(h), h, True)
            then(h)

    for h in range(LOOPED, last):
        step(h, 0, lambda i: None)
        step(h, 1, lambda i: None)
    step(last, 0, lambda i: None)
    step(last, 1, finish)

    pltpu.make_async_copy(back, back, ret_recv).wait()

    got = back[...].reshape(CHIPS, LANES)
    high = got.astype(jnp.bfloat16)
    rest = got - high.astype(jnp.float32)
    low = rest.astype(jnp.bfloat16)
    spread = lax.dot_general(
        jnp.concatenate([high, low], axis=0), onehot[...], (((0,), (0,)), ((), ())),
        preferred_element_type=jnp.float32,
    )
    place = far_z * CAP + rank
    chosen = place == lax.broadcasted_iota(jnp.int32, (LANES, rows), 0)
    out_ref[...] = jnp.sum(jnp.where(chosen, spread, 0.0), axis=0, keepdims=True)

    sent = pl.ds(0, (CHIPS - 1) * CAP)
    pltpu.make_async_copy(send.at[sent], send.at[sent], send_sem).wait()
    half = pl.ds(0, PLANE * GRP)
    pltpu.make_async_copy(pool.at[half], pool.at[half], fwd_send).wait()
    others = pl.ds(0, CHIPS - 1)
    pltpu.make_async_copy(back.at[others], back.at[others], ret_send).wait()


def on_device(embeddings, cluster_of):
    rows, features = embeddings.shape
    slots = CHIPS * CAP
    nearest = pl.pallas_call(
        kernel,
        out_shape=jax.ShapeDtypeStruct((1, rows), jnp.float32),
        in_specs=[pl.BlockSpec(memory_space=pltpu.HBM)] * 2,
        out_specs=pl.BlockSpec(memory_space=pltpu.VMEM),
        scratch_shapes=[
            pltpu.VMEM((rows, features), jnp.bfloat16),
            pltpu.VMEM((1, rows), jnp.int32),
            pltpu.VMEM((slots, features), jnp.bfloat16),
            pltpu.VMEM((2 * slots, features), jnp.bfloat16),
            pltpu.VMEM((8, slots), jnp.float32),
            pltpu.VMEM((PLANE, 1, LANES), jnp.float32),
            pltpu.VMEM((CHIPS, 1, LANES), jnp.float32),
            pltpu.VMEM((2 * CHIPS, rows), jnp.bfloat16),
            pltpu.SemaphoreType.DMA((4,)),
            pltpu.SemaphoreType.DMA,
            pltpu.SemaphoreType.DMA,
            pltpu.SemaphoreType.DMA((PLANE,)),
            pltpu.SemaphoreType.DMA,
            pltpu.SemaphoreType.DMA((PLANE,)),
            pltpu.SemaphoreType.DMA,
            pltpu.SemaphoreType.DMA,
        ],
        compiler_params=pltpu.CompilerParams(
            collective_id=0, has_side_effects=True, vmem_limit_bytes=55228 << 10
        ),
        cost_estimate=pl.CostEstimate(
            flops=2 * slots * 2 * slots * features, bytes_accessed=2 * rows * features, transcendentals=0
        ),
    )(embeddings, cluster_of.reshape(1, rows))
    return nearest.reshape(rows)


def solution(mesh):
    return jax.shard_map(
        on_device,
        mesh=mesh,
        in_specs=(P(("dp", "group"), None), P(("dp", "group"), None)),
        out_specs=P(("dp", "group")),
        check_vma=False,
    )
```

```python
import jax
import jax.numpy as jnp
from jax import lax
from jax.experimental import pallas as pl
from jax.experimental.pallas import tpu as pltpu
from jax.sharding import PartitionSpec as P

MESH = pl.DeviceIdType.MESH
NZ, NX, NY = 8, 4, 4
PLANE = NX * NY
CHIPS = NZ * PLANE
CAP = 16
GRP = NZ * CAP
PAIR = 2 * GRP
BOTH = 2 * PAIR
PAIRS = PLANE // 2
EARLY = 1
LOOPED = 6
BESIDE = 4
LEAD = 0.25
EMPTY = 4.0
LOW = -1e30
LANES = 128


def steps(r):
    p = PLANE - 1 - r // NZ
    return r % NZ, p // NY, p % NY


def hops(r):
    return sum(min(a, n - a) for a, n in zip(steps(r), (NZ, NX, NY)))


SELF = (PLANE - 1) * NZ
SEND_ORDER = sorted(range(CHIPS), key=lambda s: (s // NZ - LEAD * min(s % NZ, NZ - s % NZ), s))
OTHERS = [s for s in range(CHIPS) if s != SELF]


def kernel(
    emb_hbm, lab_hbm, out_ref,
    emb, lab, send, pool, acc, res, back, onehot,
    emb_sem, lab_sem, send_sem, recv_sem, fwd_send, fwd_recv, ret_send, ret_recv,
):
    dp = lax.axis_index("dp")
    y = lax.axis_index("group")
    z, x, core = dp // (2 * NX), (dp // 2) % NX, dp % 2
    rows = emb.shape[0]
    quarter = rows // 4

    def loading(i):
        at = pl.ds(i * quarter, quarter)
        return pltpu.make_async_copy(emb_hbm.at[at], emb.at[at], emb_sem.at[i])

    labels = pltpu.make_async_copy(lab_hbm, lab, lab_sem)
    labels.start()
    for i in range(4):
        loading(i).start()

    sign = 1 - 2 * core
    z_ahead = [((z + sign * d + NZ) % NZ) * (2 * NX) + core for d in range(NZ)]
    x_ahead = [((x + sign * d + NX) % NX) * 2 for d in range(NX)]
    y_ahead = [(y + sign * d + NY) % NY for d in range(NY)]

    def ahead(s):
        dz, dx, dy = steps(s)
        return (z_ahead[dz] + x_ahead[dx], y_ahead[dy])

    def behind(s):
        dz, dx, dy = steps(s)
        return (z_ahead[-dz] + x_ahead[-dx], y_ahead[-dy])

    sibling = ((z * NX + x) * 2 + 1 - core, y)

    barrier = pltpu.get_barrier_semaphore()

    for s in sorted(OTHERS, key=lambda s: -hops(s)):
        pl.semaphore_signal(barrier, inc=1, device_id=ahead(s), device_id_type=MESH)
    pl.semaphore_signal(barrier, inc=1, device_id=sibling, device_id_type=MESH)

    labels.wait()
    label = lab[...]
    far_z = (sign * (label % NZ - z) + NZ) % NZ
    far_x = (sign * (label // (NZ * NY) - x) + NX) % NX
    far_y = (sign * ((label // NZ) % NY - y) + NY) % NY
    chip = (PLANE - 1 - far_x * NY - far_y) * NZ + far_z
    hot = chip == lax.broadcasted_iota(jnp.int32, (CHIPS, rows), 0)
    ones = hot.astype(jnp.bfloat16)
    row = lax.broadcasted_iota(jnp.int32, (LANES, 2 * LANES), 0)
    col = lax.broadcasted_iota(jnp.int32, (LANES, 2 * LANES), 1)
    before = ((row < col) | (col >= LANES)).astype(jnp.bfloat16)
    ranks = []
    carry = jnp.zeros((CHIPS, LANES), jnp.float32)
    for t in range(rows // LANES):
        at = slice(t * LANES, (t + 1) * LANES)
        both = jnp.dot(ones[:, at], before, preferred_element_type=jnp.float32)
        earlier = jnp.where(hot[:, at], both[:, :LANES] + carry, 0.0)
        carry = carry + both[:, LANES:]
        ranks.append(jnp.sum(earlier, axis=0, keepdims=True))
    rank = jnp.concatenate(ranks, axis=1).astype(jnp.int32)
    position = chip * CAP + rank

    acc[...] = jnp.full_like(acc, -1.0)

    for i in range(4):
        loading(i).wait()

    def dispatch(h):
        base = h * PAIR
        pick = position == base + lax.broadcasted_iota(jnp.int32, (PAIR, rows), 0)
        chosen = jnp.where(pick, 1.0, 0.0)
        filled = jnp.sum(chosen, axis=1, keepdims=True)
        wide = jnp.dot(chosen.astype(jnp.bfloat16), emb[...], preferred_element_type=jnp.float32)
        total = jnp.sum(wide * wide, axis=1, keepdims=True)
        wide = wide * (1.0 / jnp.sqrt(total + 1e-06))
        lane = lax.broadcasted_iota(jnp.int32, (PAIR, LANES), 1)
        mark = jnp.where((lane == 0) & (filled == 0.0), EMPTY, 0.0)
        send[pl.ds(base, PAIR), :LANES] = (wide[:, :LANES] + mark).astype(jnp.bfloat16)
        send[pl.ds(base, PAIR), LANES:] = wide[:, LANES:].astype(jnp.bfloat16)

    def landing(s):
        return pl.ds((s // (2 * NZ)) * BOTH + s % (2 * NZ) * CAP, CAP)

    def outgoing(s):
        src, dst = pl.ds(s * CAP, CAP), landing(s)
        return pltpu.make_async_remote_copy(
            src_ref=send.at[src], dst_ref=pool.at[dst], send_sem=send_sem, recv_sem=recv_sem.at[s // NZ],
            device_id=ahead(s), device_id_type=MESH,
        )

    for h in range(EARLY):
        dispatch(h)

    pl.semaphore_wait(barrier, CHIPS)

    ready = EARLY
    for s in SEND_ORDER:
        if s // (2 * NZ) == ready:
            dispatch(ready)
            ready += 1
        if s == SELF:
            pltpu.make_async_copy(
                send.at[pl.ds(s * CAP, CAP)], pool.at[landing(s)], recv_sem.at[s // NZ]
            ).start()
        else:
            outgoing(s).start()

    onehot[:CHIPS] = ones
    onehot[CHIPS:] = ones

    def mine(h, odd):
        return pl.ds(pl.multiple_of(h * BOTH + odd * GRP, GRP), GRP)

    def theirs(h, odd):
        return pl.ds(pl.multiple_of(h * BOTH + PAIR + odd * GRP, GRP), GRP)

    def forward(h, odd):
        g = 2 * h + odd
        return pltpu.make_async_remote_copy(
            src_ref=pool.at[mine(h, odd)], dst_ref=pool.at[theirs(h, odd)],
            send_sem=fwd_send, recv_sem=fwd_recv.at[g], device_id=sibling, device_id_type=MESH,
        )

    def arrive(h, odd):
        at = mine(h, odd)
        pltpu.make_async_copy(pool.at[at], pool.at[at], recv_sem.at[2 * h + odd]).wait()

    def meet(other, i, same):
        own = pool[pl.ds(pl.multiple_of(i * BOTH, BOTH), PAIR), :]
        score = lax.dot_general(other, own, (((1,), (1,)), ((), ())), preferred_element_type=jnp.float32)
        score = score + jnp.where(other[:, 0:1].astype(jnp.float32) > 2.0, LOW, 0.0)
        if same:
            one = lax.broadcasted_iota(jnp.int32, score.shape, 0)
            two = lax.broadcasted_iota(jnp.int32, score.shape, 1)
            score = jnp.where(one == two, LOW, score)
        best = jnp.max(score.reshape(score.shape[0] // 8, 8, PAIR), axis=0)
        at = pl.ds(pl.multiple_of(i * PAIR, PAIR), PAIR)
        acc[:, at] = jnp.maximum(acc[:, at], best)

    def whole(h):
        return pool[pl.ds(pl.multiple_of(h * BOTH, BOTH), BOTH), :]

    def newest(h, odd):
        return jnp.concatenate([pool[mine(h, odd), :], pool[theirs(h, odd), :]], axis=0)

    def cross(h, i):
        meet(whole(i), h, False)
        meet(whole(h), i, False)

    @pl.loop(0, LOOPED)
    def _(h):
        for odd in range(2):
            arrive(h, odd)
            forward(h, odd).start()
        for odd in range(2):
            forward(h, odd).wait_recv()

        @pl.loop(0, h // 2)
        def _(k):
            cross(h, 2 * k)
            cross(h, 2 * k + 1)

        @pl.loop(0, h % 2)
        def _(k):
            cross(h, h - 1)

        meet(whole(h), h, True)

    last = PAIRS - 1

    def returning(s):
        return pltpu.make_async_remote_copy(
            src_ref=res.at[s // NZ], dst_ref=back.at[s], send_sem=ret_send, recv_sem=ret_recv,
            device_id=behind(s), device_id_type=MESH,
        )

    def finish(pairs):
        for i in pairs:
            best = jnp.max(acc[:, i * PAIR:(i + 1) * PAIR], axis=0, keepdims=True)
            for odd in range(2):
                res[2 * i + odd] = best[:, odd * LANES:(odd + 1) * LANES]
        slots = [s for i in pairs for s in range(2 * NZ * i, 2 * NZ * (i + 1))]
        for s in sorted(slots, key=lambda s: -hops(s)):
            if s == SELF:
                pltpu.make_async_copy(res.at[s // NZ], back.at[s], ret_recv).start()
            else:
                returning(s).start()

    def step(h, odd, then):
        arrive(h, odd)
        forward(h, odd).start()
        if odd:
            for j in range(min(h, BESIDE)):
                meet(whole(j), h, False)
        forward(h, odd).wait_recv()
        for i in range(h):
            meet(newest(h, odd), i, False)
        then(range(h))
        if odd:
            for j in range(BESIDE, h):
                meet(whole(j), h, False)
            meet(whole(h), h, True)
            then([h])

    for h in range(LOOPED, last):
        step(h, 0, lambda pairs: None)
        step(h, 1, lambda pairs: None)
    step(last, 0, lambda pairs: None)
    step(last, 1, finish)

    pltpu.make_async_copy(back, back, ret_recv).wait()

    got = back[...].reshape(CHIPS, LANES)
    high = got.astype(jnp.bfloat16)
    rest = got - high.astype(jnp.float32)
    low = rest.astype(jnp.bfloat16)
    spread = lax.dot_general(
        jnp.concatenate([high, low], axis=0), onehot[...], (((0,), (0,)), ((), ())),
        preferred_element_type=jnp.float32,
    )
    place = far_z * CAP + rank
    chosen = place == lax.broadcasted_iota(jnp.int32, (LANES, rows), 0)
    out_ref[...] = jnp.sum(jnp.where(chosen, spread, 0.0), axis=0, keepdims=True)

    sent = pl.ds(0, (CHIPS - 1) * CAP)
    pltpu.make_async_copy(send.at[sent], send.at[sent], send_sem).wait()
    half = pl.ds(0, PLANE * GRP)
    pltpu.make_async_copy(pool.at[half], pool.at[half], fwd_send).wait()
    others = pl.ds(0, CHIPS - 1)
    pltpu.make_async_copy(back.at[others], back.at[others], ret_send).wait()


def on_device(embeddings, cluster_of):
    rows, features = embeddings.shape
    slots = CHIPS * CAP
    nearest = pl.pallas_call(
        kernel,
        out_shape=jax.ShapeDtypeStruct((1, rows), jnp.float32),
        in_specs=[pl.BlockSpec(memory_space=pltpu.HBM)] * 2,
        out_specs=pl.BlockSpec(memory_space=pltpu.VMEM),
        scratch_shapes=[
            pltpu.VMEM((rows, features), jnp.bfloat16),
            pltpu.VMEM((1, rows), jnp.int32),
            pltpu.VMEM((slots, features), jnp.bfloat16),
            pltpu.VMEM((2 * slots, features), jnp.bfloat16),
            pltpu.VMEM((8, slots), jnp.float32),
            pltpu.VMEM((PLANE, 1, LANES), jnp.float32),
            pltpu.VMEM((CHIPS, 1, LANES), jnp.float32),
            pltpu.VMEM((2 * CHIPS, rows), jnp.bfloat16),
            pltpu.SemaphoreType.DMA((4,)),
            pltpu.SemaphoreType.DMA,
            pltpu.SemaphoreType.DMA,
            pltpu.SemaphoreType.DMA((PLANE,)),
            pltpu.SemaphoreType.DMA,
            pltpu.SemaphoreType.DMA((PLANE,)),
            pltpu.SemaphoreType.DMA,
            pltpu.SemaphoreType.DMA,
        ],
        compiler_params=pltpu.CompilerParams(
            collective_id=0, has_side_effects=True, vmem_limit_bytes=55228 << 10
        ),
        cost_estimate=pl.CostEstimate(
            flops=2 * slots * 2 * slots * features, bytes_accessed=2 * rows * features, transcendentals=0
        ),
    )(embeddings, cluster_of.reshape(1, rows))
    return nearest.reshape(rows)


def solution(mesh):
    return jax.shard_map(
        on_device,
        mesh=mesh,
        in_specs=(P(("dp", "group"), None), P(("dp", "group"), None)),
        out_specs=P(("dp", "group")),
        check_vma=False,
    )
```

```python
import jax
import jax.numpy as jnp
from jax import lax
from jax.experimental import pallas as pl
from jax.experimental.pallas import tpu as pltpu
from jax.sharding import PartitionSpec as P

MESH = pl.DeviceIdType.MESH
NZ, NX, NY = 8, 4, 4
PLANE = NX * NY
CHIPS = NZ * PLANE
CAP = 16
GRP = NZ * CAP
PAIR = 2 * GRP
BOTH = 2 * PAIR
PAIRS = PLANE // 2
LOOPED = 6
BESIDE = 4
LEAD = 0.25
EMPTY = 4.0
LOW = -1e30
LANES = 128


def steps(r):
    p = PLANE - 1 - r // NZ
    return r % NZ, p // NY, p % NY


def hops(r):
    return sum(min(a, n - a) for a, n in zip(steps(r), (NZ, NX, NY)))


SELF = (PLANE - 1) * NZ
SEND_ORDER = sorted(range(CHIPS), key=lambda s: (s // NZ - LEAD * min(s % NZ, NZ - s % NZ), s))
OTHERS = [s for s in range(CHIPS) if s != SELF]


def kernel(
    emb_hbm, lab_hbm, out_ref,
    emb, lab, send, pool, acc, res, back, onehot,
    emb_sem, lab_sem, send_sem, recv_sem, fwd_send, fwd_recv, ret_send, ret_recv,
):
    dp = lax.axis_index("dp")
    y = lax.axis_index("group")
    z, x, core = dp // (2 * NX), (dp // 2) % NX, dp % 2
    rows = emb.shape[0]
    quarter = rows // 4

    def loading(i):
        at = pl.ds(i * quarter, quarter)
        return pltpu.make_async_copy(emb_hbm.at[at], emb.at[at], emb_sem.at[i])

    labels = pltpu.make_async_copy(lab_hbm, lab, lab_sem)
    labels.start()
    for i in range(4):
        loading(i).start()

    sign = 1 - 2 * core
    z_ahead = [((z + sign * d + NZ) % NZ) * (2 * NX) + core for d in range(NZ)]
    x_ahead = [((x + sign * d + NX) % NX) * 2 for d in range(NX)]
    y_ahead = [(y + sign * d + NY) % NY for d in range(NY)]

    def ahead(s):
        dz, dx, dy = steps(s)
        return (z_ahead[dz] + x_ahead[dx], y_ahead[dy])

    def behind(s):
        dz, dx, dy = steps(s)
        return (z_ahead[-dz] + x_ahead[-dx], y_ahead[-dy])

    sibling = ((z * NX + x) * 2 + 1 - core, y)

    barrier = pltpu.get_barrier_semaphore()

    for s in sorted(OTHERS, key=lambda s: -hops(s)):
        pl.semaphore_signal(barrier, inc=1, device_id=ahead(s), device_id_type=MESH)
    pl.semaphore_signal(barrier, inc=1, device_id=sibling, device_id_type=MESH)

    labels.wait()
    label = lab[...]
    far_z = (sign * (label % NZ - z) + NZ) % NZ
    far_x = (sign * (label // (NZ * NY) - x) + NX) % NX
    far_y = (sign * ((label // NZ) % NY - y) + NY) % NY
    chip = (PLANE - 1 - far_x * NY - far_y) * NZ + far_z
    hot = chip == lax.broadcasted_iota(jnp.int32, (CHIPS, rows), 0)
    ones = hot.astype(jnp.bfloat16)
    row = lax.broadcasted_iota(jnp.int32, (LANES, 2 * LANES), 0)
    col = lax.broadcasted_iota(jnp.int32, (LANES, 2 * LANES), 1)
    before = ((row < col) | (col >= LANES)).astype(jnp.bfloat16)
    ranks = []
    carry = jnp.zeros((CHIPS, LANES), jnp.float32)
    for t in range(rows // LANES):
        at = slice(t * LANES, (t + 1) * LANES)
        both = jnp.dot(ones[:, at], before, preferred_element_type=jnp.float32)
        earlier = jnp.where(hot[:, at], both[:, :LANES] + carry, 0.0)
        carry = carry + both[:, LANES:]
        ranks.append(jnp.sum(earlier, axis=0, keepdims=True))
    rank = jnp.concatenate(ranks, axis=1).astype(jnp.int32)
    position = chip * CAP + rank

    acc[...] = jnp.full_like(acc, -1.0)

    for i in range(4):
        loading(i).wait()

    def dispatch(base, count):
        pick = position == base + lax.broadcasted_iota(jnp.int32, (count, rows), 0)
        chosen = jnp.where(pick, 1.0, 0.0)
        filled = jnp.sum(chosen, axis=1, keepdims=True)
        wide = jnp.dot(chosen.astype(jnp.bfloat16), emb[...], preferred_element_type=jnp.float32)
        total = jnp.sum(wide * wide, axis=1, keepdims=True)
        wide = wide * (1.0 / jnp.sqrt(total + 1e-06))
        lane = lax.broadcasted_iota(jnp.int32, (count, LANES), 1)
        mark = jnp.where((lane == 0) & (filled == 0.0), EMPTY, 0.0)
        send[pl.ds(base, count), :LANES] = (wide[:, :LANES] + mark).astype(jnp.bfloat16)
        send[pl.ds(base, count), LANES:] = wide[:, LANES:].astype(jnp.bfloat16)

    def landing(s):
        return pl.ds((s // (2 * NZ)) * BOTH + s % (2 * NZ) * CAP, CAP)

    def outgoing(s):
        src, dst = pl.ds(s * CAP, CAP), landing(s)
        return pltpu.make_async_remote_copy(
            src_ref=send.at[src], dst_ref=pool.at[dst], send_sem=send_sem, recv_sem=recv_sem.at[s // NZ],
            device_id=ahead(s), device_id_type=MESH,
        )

    dispatch(0, GRP)

    pl.semaphore_wait(barrier, CHIPS)

    ready = GRP
    for s in SEND_ORDER:
        if s * CAP >= ready:
            count = GRP if ready == GRP else PAIR
            dispatch(ready, count)
            ready += count
        if s == SELF:
            pltpu.make_async_copy(
                send.at[pl.ds(s * CAP, CAP)], pool.at[landing(s)], recv_sem.at[s // NZ]
            ).start()
        else:
            outgoing(s).start()

    onehot[:CHIPS] = ones
    onehot[CHIPS:] = ones

    def mine(h, odd):
        return pl.ds(pl.multiple_of(h * BOTH + odd * GRP, GRP), GRP)

    def theirs(h, odd):
        return pl.ds(pl.multiple_of(h * BOTH + PAIR + odd * GRP, GRP), GRP)

    def forward(h, odd):
        g = 2 * h + odd
        return pltpu.make_async_remote_copy(
            src_ref=pool.at[mine(h, odd)], dst_ref=pool.at[theirs(h, odd)],
            send_sem=fwd_send, recv_sem=fwd_recv.at[g], device_id=sibling, device_id_type=MESH,
        )

    def arrive(h, odd):
        at = mine(h, odd)
        pltpu.make_async_copy(pool.at[at], pool.at[at], recv_sem.at[2 * h + odd]).wait()

    def meet(other, i, same):
        own = pool[pl.ds(pl.multiple_of(i * BOTH, BOTH), PAIR), :]
        score = lax.dot_general(other, own, (((1,), (1,)), ((), ())), preferred_element_type=jnp.float32)
        score = score + jnp.where(other[:, 0:1].astype(jnp.float32) > 2.0, LOW, 0.0)
        if same:
            one = lax.broadcasted_iota(jnp.int32, score.shape, 0)
            two = lax.broadcasted_iota(jnp.int32, score.shape, 1)
            score = jnp.where(one == two, LOW, score)
        best = jnp.max(score.reshape(score.shape[0] // 8, 8, PAIR), axis=0)
        at = pl.ds(pl.multiple_of(i * PAIR, PAIR), PAIR)
        acc[:, at] = jnp.maximum(acc[:, at], best)

    def whole(h):
        return pool[pl.ds(pl.multiple_of(h * BOTH, BOTH), BOTH), :]

    def newest(h, odd):
        return jnp.concatenate([pool[mine(h, odd), :], pool[theirs(h, odd), :]], axis=0)

    def cross(h, i):
        meet(whole(i), h, False)
        meet(whole(h), i, False)

    @pl.loop(0, LOOPED)
    def _(h):
        for odd in range(2):
            arrive(h, odd)
            forward(h, odd).start()
        for odd in range(2):
            forward(h, odd).wait_recv()

        @pl.loop(0, h // 2)
        def _(k):
            cross(h, 2 * k)
            cross(h, 2 * k + 1)

        @pl.loop(0, h % 2)
        def _(k):
            cross(h, h - 1)

        meet(whole(h), h, True)

    last = PAIRS - 1

    def returning(s):
        return pltpu.make_async_remote_copy(
            src_ref=res.at[s // NZ], dst_ref=back.at[s], send_sem=ret_send, recv_sem=ret_recv,
            device_id=behind(s), device_id_type=MESH,
        )

    def finish(pairs):
        for i in pairs:
            best = jnp.max(acc[:, i * PAIR:(i + 1) * PAIR], axis=0, keepdims=True)
            for odd in range(2):
                res[2 * i + odd] = best[:, odd * LANES:(odd + 1) * LANES]
        slots = [s for i in pairs for s in range(2 * NZ * i, 2 * NZ * (i + 1))]
        for s in sorted(slots, key=lambda s: -hops(s)):
            if s == SELF:
                pltpu.make_async_copy(res.at[s // NZ], back.at[s], ret_recv).start()
            else:
                returning(s).start()

    def step(h, odd, then):
        arrive(h, odd)
        forward(h, odd).start()
        if odd:
            for j in range(min(h, BESIDE)):
                meet(whole(j), h, False)
        forward(h, odd).wait_recv()
        for i in range(h):
            meet(newest(h, odd), i, False)
        then(range(h))
        if odd:
            for j in range(BESIDE, h):
                meet(whole(j), h, False)
            meet(whole(h), h, True)
            then([h])

    for h in range(LOOPED, last):
        step(h, 0, lambda pairs: None)
        step(h, 1, lambda pairs: None)
    step(last, 0, lambda pairs: None)
    step(last, 1, finish)

    pltpu.make_async_copy(back, back, ret_recv).wait()

    got = back[...].reshape(CHIPS, LANES)
    high = got.astype(jnp.bfloat16)
    rest = got - high.astype(jnp.float32)
    low = rest.astype(jnp.bfloat16)
    spread = lax.dot_general(
        jnp.concatenate([high, low], axis=0), onehot[...], (((0,), (0,)), ((), ())),
        preferred_element_type=jnp.float32,
    )
    place = far_z * CAP + rank
    chosen = place == lax.broadcasted_iota(jnp.int32, (LANES, rows), 0)
    out_ref[...] = jnp.sum(jnp.where(chosen, spread, 0.0), axis=0, keepdims=True)

    sent = pl.ds(0, (CHIPS - 1) * CAP)
    pltpu.make_async_copy(send.at[sent], send.at[sent], send_sem).wait()
    half = pl.ds(0, PLANE * GRP)
    pltpu.make_async_copy(pool.at[half], pool.at[half], fwd_send).wait()
    others = pl.ds(0, CHIPS - 1)
    pltpu.make_async_copy(back.at[others], back.at[others], ret_send).wait()


def on_device(embeddings, cluster_of):
    rows, features = embeddings.shape
    slots = CHIPS * CAP
    nearest = pl.pallas_call(
        kernel,
        out_shape=jax.ShapeDtypeStruct((1, rows), jnp.float32),
        in_specs=[pl.BlockSpec(memory_space=pltpu.HBM)] * 2,
        out_specs=pl.BlockSpec(memory_space=pltpu.VMEM),
        scratch_shapes=[
            pltpu.VMEM((rows, features), jnp.bfloat16),
            pltpu.VMEM((1, rows), jnp.int32),
            pltpu.VMEM((slots, features), jnp.bfloat16),
            pltpu.VMEM((2 * slots, features), jnp.bfloat16),
            pltpu.VMEM((8, slots), jnp.float32),
            pltpu.VMEM((PLANE, 1, LANES), jnp.float32),
            pltpu.VMEM((CHIPS, 1, LANES), jnp.float32),
            pltpu.VMEM((2 * CHIPS, rows), jnp.bfloat16),
            pltpu.SemaphoreType.DMA((4,)),
            pltpu.SemaphoreType.DMA,
            pltpu.SemaphoreType.DMA,
            pltpu.SemaphoreType.DMA((PLANE,)),
            pltpu.SemaphoreType.DMA,
            pltpu.SemaphoreType.DMA((PLANE,)),
            pltpu.SemaphoreType.DMA,
            pltpu.SemaphoreType.DMA,
        ],
        compiler_params=pltpu.CompilerParams(
            collective_id=0, has_side_effects=True, vmem_limit_bytes=55228 << 10
        ),
        cost_estimate=pl.CostEstimate(
            flops=2 * slots * 2 * slots * features, bytes_accessed=2 * rows * features, transcendentals=0
        ),
    )(embeddings, cluster_of.reshape(1, rows))
    return nearest.reshape(rows)


def solution(mesh):
    return jax.shard_map(
        on_device,
        mesh=mesh,
        in_specs=(P(("dp", "group"), None), P(("dp", "group"), None)),
        out_specs=P(("dp", "group")),
        check_vma=False,
    )
```
